32 devices in a mesh: tmpl: 1, freq: 32 (over z, y, x, core).
Axes of the slice: x: 2, y: 2, z: 4, core: 2. Of those that a mesh axis runs over, the one named last changes fastest.
Arguments:
- strain: float32 [512, 512], P('freq'), may hold values from -6 to 6
- inv_asd: float32 [512, 512], P('freq'), may hold values from 0.25 to 4
- spectra: bfloat16 [512, 4, 2, 512], P('freq', 'tmpl'), may hold values from -6 to 6
- cutoff: int32 [4], P('tmpl'), may hold values from 64 to 256
Outputs:
- filter_series: float32 [4, 2, 512, 512], P('tmpl', None, 'freq')
- peak_power: float32 [512, 512], P('freq')
The draws below stay inside these ranges and needn't reach their ends.
All inputs are finite; a program needn't handle non-finite values.
Results may differ from the reference program's by a relative error of at most 0.0051.
Values may be sent and summed in bfloat16 or wider, within the bound.
No kernel may reach another device: no remote copies, remote signals or barrier semaphores. Data moves between devices by JAX's collectives and lax.ppermute only.
A program may use at most 64 MiB of HBM per device.

```python
import math
import jax
import jax.numpy as jnp
from jax import lax

N1 = 512
TEMPLATES = 4


def with_ends(result, stream_key, low, top_value):
    longest = result.shape.index(max(result.shape))
    spots = []
    for shift in (0, 1):
        where = [jax.random.randint(jax.random.fold_in(stream_key, axis), (), 0, length) for axis, length in enumerate(result.shape)]
        where[longest] = (where[longest] + shift) % result.shape[longest]
        spots.append(tuple(where))
    return result.at[spots[0]].set(low).at[spots[1]].set(top_value)


def block_levels(rng, shape, split, low, top_value):
    def one(position, blocks):
        draws = jax.random.uniform(jax.random.fold_in(jax.random.fold_in(rng, 6), position), (blocks,), jnp.float32, low / len(split), top_value / len(split))
        return jnp.repeat(jnp.exp(draws), shape[position] // blocks).reshape((-1,) + (1,) * (len(shape) - position - 1))

    level = one(*split[0])
    for cut in split[1:]:
        level = level * one(*cut)
    return level


def bell_draw(rng, extent, width, limit, shards=(), held_as=jnp.bfloat16):
    array = width * jax.random.normal(rng, extent, jnp.float32)
    if shards:
        array = array * block_levels(rng, extent, shards, -0.22, 0.18)
    return jnp.clip(array, -limit, limit).astype(held_as)


def setup_inputs(seed: int = 0) -> dict:
    streams_of = jax.random.split(jax.random.key(seed), 5)
    return {
        "strain": bell_draw(streams_of[0], (N1, N1), 1.0, 6.0, ((0, 32),), jnp.float32),
        "inv_asd": jnp.clip(jnp.exp(math.log(4.0) - 2.7725887 * jax.random.uniform(streams_of[1], (N1, N1), jnp.float32) ** block_levels(streams_of[1], (N1, N1), ((0, 32),), -0.2, 0.2)), 0.25, 4.0),
        "spectra": bell_draw(streams_of[2], (N1, TEMPLATES, 2, N1), 1.0, 6.0, ((0, 32),)),
        "cutoff": with_ends(jax.random.randint(streams_of[3], (TEMPLATES,), N1 // 8, N1 // 2 + 1), jax.random.fold_in(streams_of[3], 1), N1 // 8, (N1 // 2 + 1) - 1).astype(jnp.int32),
    }


def angle_table(left, right, modulus):
    product = (left[:, None] * right[None, :]) % modulus
    return (2.0 * math.pi / modulus) * product.astype(jnp.float32)


def inverse_table(side_size):
    positions = jnp.arange(side_size, dtype=jnp.int32)
    angles = angle_table(positions, positions, side_size)
    cosines = jnp.cos(angles)
    sine_part = jnp.sin(angles)
    stacked = jnp.stack([jnp.stack([cosines, sine_part]), jnp.stack([-sine_part, cosines])])
    return stacked.astype(jnp.bfloat16)


def reference(strain, inv_asd, spectra, cutoff):
    side_size = N1
    total_size = side_size * side_size
    spectrum_full = jnp.fft.fft(strain.reshape(-1)).reshape(side_size, side_size).T
    white_real = jnp.real(spectrum_full).astype(jnp.float32) * inv_asd
    white_imag = jnp.imag(spectrum_full).astype(jnp.float32) * inv_asd
    base_table = inverse_table(side_size)
    section_table = jnp.transpose(base_table, (0, 2, 1, 3)).astype(jnp.float32)
    last_table = jnp.transpose(base_table, (2, 0, 1, 3)).astype(jnp.float32)
    positions = jnp.arange(side_size, dtype=jnp.int32)
    twist_angle = angle_table(positions, positions, total_size)
    twist_cos = jnp.cos(twist_angle)[:, :, None]
    twist_sin = jnp.sin(twist_angle)[:, :, None]
    group_size = math.gcd(8, TEMPLATES)

    def one_block(peak_power, block_index):
        chosen = lax.dynamic_slice_in_dim(spectra, block_index * group_size, group_size, 1).astype(jnp.float32)
        limits = lax.dynamic_slice_in_dim(cutoff, block_index * group_size, group_size, 0)
        band_mask = (positions[None, :] < limits[:, None]).astype(jnp.float32)[None]
        spec_real = chosen[:, :, 0]
        spec_imag = chosen[:, :, 1]
        prod_real = (white_real[:, None] * spec_real + white_imag[:, None] * spec_imag) * band_mask
        prod_imag = (white_imag[:, None] * spec_real - white_real[:, None] * spec_imag) * band_mask
        product = jnp.stack([prod_real, prod_imag], 2).astype(jnp.bfloat16)
        turned = jnp.einsum("ktcj,cjdm->kmtd", product.astype(jnp.float32), section_table)
        real_part = turned[..., 0]
        imag_part = turned[..., 1]
        rotated = jnp.stack([real_part * twist_cos - imag_part * twist_sin, real_part * twist_sin + imag_part * twist_cos], -1).astype(jnp.bfloat16)
        series = jnp.einsum("kmtc,kcdn->tdmn", rotated.astype(jnp.float32), last_table) * (1.0 / total_size)
        power_sum = series[:, 0] ** 2 + series[:, 1] ** 2
        return jnp.maximum(peak_power, jnp.max(power_sum, axis=0)), series

    start_peak = jnp.zeros((side_size, side_size), jnp.float32)
    peak_power, blocks = lax.scan(one_block, start_peak, jnp.arange(TEMPLATES // group_size, dtype=jnp.int32))
    filter_series = blocks.reshape(TEMPLATES, 2, side_size, side_size)
    return filter_series, peak_power
```

```python
import functools

import jax
import jax.numpy as jnp
import ml_dtypes
import numpy as np
from jax import lax
from jax.experimental import pallas as pl
from jax.experimental.pallas import tpu as pltpu
from jax.sharding import PartitionSpec as P

BAND = 256


def angles(left, right, modulus):
    return 2.0 * np.pi / modulus * (left[:, None] * right[None, :] % modulus)


def split(table):
    high = table.astype(ml_dtypes.bfloat16)
    low = (table - high.astype(np.float64)).astype(ml_dtypes.bfloat16)
    return high, low


def forward_table(side, rows):
    count = side // rows
    positions = np.arange(side)
    angle = angles(positions, positions, side)
    core = positions // rows % 2
    result = []
    for device in range(count):
        order = np.concatenate([positions[core == device % 2], positions[core != device % 2]])
        part = angle[device * rows : (device + 1) * rows][:, order]
        high, low = split(np.concatenate([np.cos(part), -np.sin(part)]))
        result.append(np.concatenate([high, low]))
    return np.stack(result)


def dot(left, right):
    return jnp.dot(left, right, preferred_element_type=jnp.float32)


def spread(slots, rows):
    count = len(slots)
    lane = lax.broadcasted_iota(jnp.int32, slots[0].shape, 1)
    lanes = slots[0].shape[1]
    bit = 1
    while bit < count:
        step = rows * bit
        keep = (lane // step) % 2 == 0
        after = list(slots)
        for low in range(count):
            if low & bit:
                continue
            high = low | bit
            after[low] = jnp.where(keep, slots[low], pltpu.roll(slots[high], step, 1))
            after[high] = jnp.where(keep, pltpu.roll(slots[low], lanes - step, 1), slots[high])
        slots = after
        bit *= 2
    return slots


def middle_kernel(own, other, forward, twist, column_high, column_low, inv_asd, spectra, cutoff, section_table, out):
    rows, side = twist.shape[1:]
    templ_count = spectra.shape[0]
    half = side // 2
    first = dot(forward[0, :, :half], own[...]) + dot(forward[0, :, half:], other[...])
    first = first[: 2 * rows] + first[2 * rows :]
    first_real, first_imag = first[:rows], first[rows:]
    twist_cos, twist_sin = twist[0], twist[1]
    turned = jnp.concatenate(
        [first_real * twist_cos + first_imag * twist_sin, first_imag * twist_cos - first_real * twist_sin], 0
    )
    high = turned.astype(jnp.bfloat16)
    low = (turned - high.astype(jnp.float32)).astype(jnp.bfloat16)
    both = dot(jnp.concatenate([high, low], 0), column_high[...])
    second = both[: 2 * rows] + both[2 * rows :] + dot(high, column_low[...])
    asd = inv_asd[:, :BAND]
    white_real = (second[:rows, :BAND] + second[rows:, BAND:]) * asd
    white_imag = (second[rows:, :BAND] - second[:rows, BAND:]) * asd
    band = lax.broadcasted_iota(jnp.int32, (rows, BAND), 1)
    product = []
    for part in range(2):
        for templ in range(templ_count):
            spec_real = spectra[templ, 0, :, :BAND].astype(jnp.float32)
            spec_imag = spectra[templ, 1, :, :BAND].astype(jnp.float32)
            if part == 0:
                value = white_real * spec_real + white_imag * spec_imag
            else:
                value = white_imag * spec_real - white_real * spec_imag
            product.append(jnp.where(band < cutoff[templ], value, 0.0).astype(jnp.bfloat16))
    turned = dot(jnp.concatenate(product, 0), section_table[...])
    group = templ_count * rows
    real_part = turned[:group, :side] - turned[group:, side:]
    imag_part = turned[:group, side:] + turned[group:, :side]
    slots = []
    for templ in range(templ_count):
        here = slice(templ * rows, (templ + 1) * rows)
        slots.append(real_part[here] * twist_cos - imag_part[here] * twist_sin)
    for templ in range(templ_count):
        here = slice(templ * rows, (templ + 1) * rows)
        slots.append(real_part[here] * twist_sin + imag_part[here] * twist_cos)
    for start in range(0, side, 128):
        pieces = spread([slot[:, start : start + 128] for slot in slots], rows)
        for place, piece in enumerate(pieces):
            out[start // rows + place] = piece.astype(jnp.bfloat16)


def last_kernel(received, table, series, peak):
    templ_count, _, rows, side = series.shape
    scale = 1.0 / (side * side)
    turned = lax.dot_general(
        received[...], table[...], (((0,), (0,)), ((), ())), preferred_element_type=jnp.float32
    )
    group = templ_count * rows
    real_part = (turned[:group, :side] - turned[group:, side:]) * scale
    imag_part = (turned[:group, side:] + turned[group:, :side]) * scale
    power = real_part * real_part + imag_part * imag_part
    best = power[:rows]
    for templ in range(templ_count):
        here = slice(templ * rows, (templ + 1) * rows)
        series[templ, 0] = real_part[here]
        series[templ, 1] = imag_part[here]
        best = jnp.maximum(best, power[here])
    peak[...] = best


def middle_plain(own, other, forward, twist, column_high, column_low, inv_asd, spectra, cutoff, section_table):
    rows, side = twist.shape[1:]
    templ_count = spectra.shape[0]
    first = dot(forward[0], jnp.concatenate([own, other], 0))
    first = first[: 2 * rows] + first[2 * rows :]
    first_real, first_imag = first[:rows], first[rows:]
    twist_cos, twist_sin = twist[0], twist[1]
    turned = jnp.concatenate(
        [first_real * twist_cos + first_imag * twist_sin, first_imag * twist_cos - first_real * twist_sin], 0
    )
    high = turned.astype(jnp.bfloat16)
    low = (turned - high.astype(jnp.float32)).astype(jnp.bfloat16)
    second = dot(high, column_high) + dot(low, column_high) + dot(high, column_low)
    asd = inv_asd[:, :BAND]
    white_real = (second[:rows, :BAND] + second[rows:, BAND:]) * asd
    white_imag = (second[rows:, :BAND] - second[:rows, BAND:]) * asd
    keep = jnp.arange(BAND, dtype=jnp.int32)[None, :] < cutoff[:, None]
    spec_real = spectra[:, 0, :, :BAND].astype(jnp.float32)
    spec_imag = spectra[:, 1, :, :BAND].astype(jnp.float32)
    product = jnp.stack([white_real * spec_real + white_imag * spec_imag, white_imag * spec_real - white_real * spec_imag])
    product = jnp.where(keep[None, :, None], product, 0.0).astype(jnp.bfloat16)
    turned = jnp.einsum("ctkj,jn->ctkn", product, section_table, preferred_element_type=jnp.float32)
    real_part = turned[0, ..., :side] - turned[1, ..., side:]
    imag_part = turned[0, ..., side:] + turned[1, ..., :side]
    rotated = jnp.stack(
        [real_part * twist_cos - imag_part * twist_sin, real_part * twist_sin + imag_part * twist_cos]
    ).astype(jnp.bfloat16)
    pieces = rotated.reshape(2, templ_count, rows, side // rows, rows)
    return jnp.transpose(pieces, (3, 2, 0, 1, 4)).reshape(side // rows, rows, -1)


def last_plain(received, table, templ_count, rows):
    side = received.shape[0]
    scale = 1.0 / (side * side)
    turned = lax.dot_general(received, table, (((0,), (0,)), ((), ())), preferred_element_type=jnp.float32)
    turned = turned.reshape(2, templ_count, rows, 2 * side)
    real_part = (turned[0, ..., :side] - turned[1, ..., side:]) * scale
    imag_part = (turned[0, ..., side:] + turned[1, ..., :side]) * scale
    series = jnp.stack([real_part, imag_part], 1)
    return series, jnp.max(real_part * real_part + imag_part * imag_part, axis=0)


def local(device_count, strain, inv_asd, spectra, cutoff):
    rows, side = strain.shape
    templ_count = spectra.shape[1]
    positions = np.arange(side)
    device = lax.axis_index("freq")
    angle = angles(positions, positions, side)
    cosines, sines = np.cos(angle), np.sin(angle)
    column_high, column_low = split(np.concatenate([cosines[:, :BAND], sines[:, :BAND]], 1))
    full_table = np.concatenate([cosines, sines], 1).astype(ml_dtypes.bfloat16)
    section_table, last_table = full_table[:BAND], full_table
    twist_angle = angles(positions, positions, side * side)
    twist_all = np.stack([np.cos(twist_angle), np.sin(twist_angle)]).astype(np.float32)
    forward = lax.dynamic_slice_in_dim(jnp.asarray(forward_table(side, rows)), device, 1, 0)
    twist = lax.dynamic_slice_in_dim(jnp.asarray(twist_all), device * rows, rows, 1)
    chips = device_count // 2
    groups = [[2 * chip + core for chip in range(chips)] for core in range(2)]
    copies = jnp.broadcast_to(strain.astype(jnp.bfloat16)[None], (chips, rows, side))
    own = lax.all_to_all(copies, "freq", 0, 0, tiled=True, axis_index_groups=groups).reshape(-1, side)
    other = lax.ppermute(own, "freq", [(i, i ^ 1) for i in range(device_count)])
    by_templ = jnp.transpose(spectra, (1, 2, 0, 3))
    args = (
        own,
        other,
        forward,
        twist,
        jnp.asarray(column_high),
        jnp.asarray(column_low),
        inv_asd,
        by_templ,
        cutoff,
        jnp.asarray(section_table),
    )
    tiles_fit = rows % 16 == 0 and 2 * templ_count * rows == 128 and side % 128 == 0
    if tiles_fit:
        vmem = pl.BlockSpec(memory_space=pltpu.VMEM)
        smem = pl.BlockSpec(memory_space=pltpu.SMEM)
        outgoing = pl.pallas_call(
            middle_kernel,
            out_shape=jax.ShapeDtypeStruct((device_count, rows, 128), jnp.bfloat16),
            in_specs=[vmem] * 8 + [smem, vmem],
            out_specs=vmem,
        )(*args)
    else:
        outgoing = middle_plain(*args)
    received = lax.all_to_all(outgoing, "freq", 0, 0, tiled=True).reshape(side, -1)
    if tiles_fit:
        series, peak = pl.pallas_call(
            last_kernel,
            out_shape=(
                jax.ShapeDtypeStruct((templ_count, 2, rows, side), jnp.float32),
                jax.ShapeDtypeStruct((rows, side), jnp.float32),
            ),
            in_specs=[vmem] * 2,
            out_specs=(vmem, vmem),
        )(received, jnp.asarray(last_table))
    else:
        series, peak = last_plain(received, jnp.asarray(last_table), templ_count, rows)
    return series, lax.pmax(peak, "tmpl")


def solution(mesh):
    in_specs = (P("freq", None), P("freq", None), P("freq", "tmpl", None, None), P("tmpl"))
    out_specs = (P("tmpl", None, "freq", None), P("freq", None))
    return jax.shard_map(
        functools.partial(local, mesh.shape["freq"]),
        mesh=mesh,
        in_specs=in_specs,
        out_specs=out_specs,
        check_vma=False,
    )
```

```python
import functools

import jax
import jax.numpy as jnp
import ml_dtypes
import numpy as np
from jax import lax
from jax.experimental import pallas as pl
from jax.experimental.pallas import tpu as pltpu
from jax.sharding import PartitionSpec as P

BAND = 256
VMEM_LIMIT = 16 << 20


def angles(left, right, modulus):
    return 2.0 * np.pi / modulus * (left[:, None] * right[None, :] % modulus)


def split(table):
    high = table.astype(ml_dtypes.bfloat16)
    low = (table - high.astype(np.float64)).astype(ml_dtypes.bfloat16)
    return high, low


def device_tables(side, rows):
    count = side // rows
    positions = np.arange(side)
    core = positions // rows % 2
    orders = [np.concatenate([positions[core == own], positions[core != own]]) for own in range(2)]
    devices = np.arange(count)
    twist = angles(devices * rows, positions, side * side)
    forward = angles(devices * rows, positions, side)
    forward = np.stack([forward[device, orders[device % 2]] for device in range(count)])
    result = [np.cos(twist), np.sin(twist), np.cos(forward), np.sin(forward)]
    for own in range(2):
        twist = angles(np.arange(rows), positions, side * side)
        forward = angles(np.arange(rows), positions, side)[:, orders[own]]
        result += [np.cos(twist), np.sin(twist), np.cos(forward), np.sin(forward)]
    return np.concatenate(result).astype(np.float32)


def transform_table(side):
    angle = angles(np.arange(side), np.arange(side), side)
    cos_high, cos_low = split(np.cos(angle))
    sin_high, sin_low = split(np.sin(angle))
    return np.concatenate([cos_high, sin_high, cos_low[:, :BAND], sin_low[:, :BAND]], 1)


def device_rows(take, count, rows):
    device = lax.axis_index("freq")

    def turn(which):
        base = 4 * count + (device % 2 * 4 + which) * rows
        row_cos, row_sin = take(which * count + device, 1), take((which + 1) * count + device, 1)
        part_cos, part_sin = take(base, rows), take(base + rows, rows)
        return row_cos * part_cos - row_sin * part_sin, row_cos * part_sin + row_sin * part_cos

    twist_cos, twist_sin = turn(0)
    forward_cos, forward_sin = turn(2)
    exact = jnp.concatenate([forward_cos, -forward_sin], 0)
    high = exact.astype(jnp.bfloat16)
    low = (exact - high.astype(jnp.float32)).astype(jnp.bfloat16)
    return twist_cos, twist_sin, jnp.concatenate([high, low], 0)


def dot(left, right):
    return jnp.dot(left, right, preferred_element_type=jnp.float32)


def spread(slots, rows):
    count = len(slots)
    lane = lax.broadcasted_iota(jnp.int32, slots[0].shape, 1)
    lanes = slots[0].shape[1]
    bit = 1
    while bit < count:
        step = rows * bit
        keep = (lane // step) % 2 == 0
        after = list(slots)
        for low in range(count):
            if low & bit:
                continue
            high = low | bit
            after[low] = jnp.where(keep, slots[low], pltpu.roll(slots[high], step, 1))
            after[high] = jnp.where(keep, pltpu.roll(slots[low], lanes - step, 1), slots[high])
        slots = after
        bit *= 2
    return slots


def prepare_kernel(turns, table, twist, forward, table_out, copied):
    copy = pltpu.make_async_copy(table, table_out, copied)
    copy.start()
    _, rows, side = twist.shape
    twist[0], twist[1], forward[...] = device_rows(lambda start, size: turns[pl.ds(start, size), :], side // rows, rows)
    copy.wait()


def middle_kernel(own, other, twist, forward, table, inv_asd, spectra, out):
    templ_count, _, rows, _ = spectra.shape
    side = own.shape[1]
    half = side // 2
    twist_cos, twist_sin = twist[0], twist[1]
    first = dot(forward[:, :half], own[...]) + dot(forward[:, half:], other[...])
    first = first[: 2 * rows] + first[2 * rows :]
    first_real, first_imag = first[:rows], first[rows:]
    turned = jnp.concatenate(
        [first_real * twist_cos + first_imag * twist_sin, first_imag * twist_cos - first_real * twist_sin], 0
    )
    high = turned.astype(jnp.bfloat16)
    low = (turned - high.astype(jnp.float32)).astype(jnp.bfloat16)
    both = jnp.concatenate([high, low], 0)
    both = [dot(both, table[:, start : start + BAND]) for start in (0, side)]
    rest = [dot(high, table[:, 2 * side + start : 2 * side + start + BAND]) for start in (0, BAND)]
    by_cos, by_sin = [x[: 2 * rows] + x[2 * rows :] + y for x, y in zip(both, rest)]
    asd = inv_asd[...]
    white_real = (by_cos[:rows] + by_sin[rows:]) * asd
    white_imag = (by_cos[rows:] - by_sin[:rows]) * asd
    product = []
    for part in range(2):
        for templ in range(templ_count):
            spec_real = spectra[templ, 0].astype(jnp.float32)
            spec_imag = spectra[templ, 1].astype(jnp.float32)
            if part == 0:
                value = white_real * spec_real + white_imag * spec_imag
            else:
                value = white_imag * spec_real - white_real * spec_imag
            product.append(value.astype(jnp.bfloat16))
    turned = dot(jnp.concatenate(product, 0), table[:BAND, : 2 * side])
    group = templ_count * rows
    real_part = turned[:group, :side] - turned[group:, side:]
    imag_part = turned[:group, side:] + turned[group:, :side]
    slots = []
    for templ in range(templ_count):
        here = slice(templ * rows, (templ + 1) * rows)
        slots.append(real_part[here] * twist_cos - imag_part[here] * twist_sin)
    for templ in range(templ_count):
        here = slice(templ * rows, (templ + 1) * rows)
        slots.append(real_part[here] * twist_sin + imag_part[here] * twist_cos)
    for start in range(0, side, 128):
        pieces = spread([slot[:, start : start + 128] for slot in slots], rows)
        for place, piece in enumerate(pieces):
            out[start // rows + place] = piece.astype(jnp.bfloat16)


def last_kernel(received, table, series, peak):
    templ_count, _, rows, side = series.shape
    scale = 1.0 / (side * side)
    turned = lax.dot_general(
        received[...], table[:, : 2 * side], (((0,), (0,)), ((), ())), preferred_element_type=jnp.float32
    )
    group = templ_count * rows
    real_part = (turned[:group, :side] - turned[group:, side:]) * scale
    imag_part = (turned[:group, side:] + turned[group:, :side]) * scale
    power = real_part * real_part + imag_part * imag_part
    best = power[:rows]
    for templ in range(templ_count):
        here = slice(templ * rows, (templ + 1) * rows)
        series[templ, 0] = real_part[here]
        series[templ, 1] = imag_part[here]
        best = jnp.maximum(best, power[here])
    peak[...] = best


def prepare_plain(turns, table, rows):
    twist_cos, twist_sin, forward = device_rows(
        lambda start, size: lax.dynamic_slice_in_dim(turns, start, size, 0), table.shape[0] // rows, rows
    )
    return jnp.stack([twist_cos, twist_sin]), forward, table


def middle_plain(own, other, twist, forward, table, inv_asd, spectra):
    templ_count, _, rows, _ = spectra.shape
    side = own.shape[1]
    twist_cos, twist_sin = twist[0], twist[1]
    first = dot(forward, jnp.concatenate([own, other], 0))
    first = first[: 2 * rows] + first[2 * rows :]
    first_real, first_imag = first[:rows], first[rows:]
    turned = jnp.concatenate(
        [first_real * twist_cos + first_imag * twist_sin, first_imag * twist_cos - first_real * twist_sin], 0
    )
    high = turned.astype(jnp.bfloat16)
    low = (turned - high.astype(jnp.float32)).astype(jnp.bfloat16)
    column_high = jnp.concatenate([table[:, :BAND], table[:, side : side + BAND]], 1)
    second = dot(high, column_high) + dot(low, column_high) + dot(high, table[:, 2 * side :])
    asd = inv_asd[...]
    white_real = (second[:rows, :BAND] + second[rows:, BAND:]) * asd
    white_imag = (second[rows:, :BAND] - second[:rows, BAND:]) * asd
    spec_real = spectra[:, 0].astype(jnp.float32)
    spec_imag = spectra[:, 1].astype(jnp.float32)
    product = jnp.stack([white_real * spec_real + white_imag * spec_imag, white_imag * spec_real - white_real * spec_imag])
    product = product.astype(jnp.bfloat16)
    turned = jnp.einsum("ctkj,jn->ctkn", product, table[:BAND, : 2 * side], preferred_element_type=jnp.float32)
    real_part = turned[0, ..., :side] - turned[1, ..., side:]
    imag_part = turned[0, ..., side:] + turned[1, ..., :side]
    rotated = jnp.stack(
        [real_part * twist_cos - imag_part * twist_sin, real_part * twist_sin + imag_part * twist_cos]
    ).astype(jnp.bfloat16)
    pieces = rotated.reshape(2, templ_count, rows, side // rows, rows)
    return jnp.transpose(pieces, (3, 2, 0, 1, 4)).reshape(side // rows, rows, -1)


def last_plain(received, table, templ_count, rows):
    side = received.shape[0]
    scale = 1.0 / (side * side)
    turned = lax.dot_general(received, table, (((0,), (0,)), ((), ())), preferred_element_type=jnp.float32)
    turned = turned[:, : 2 * side].reshape(2, templ_count, rows, 2 * side)
    real_part = (turned[0, ..., :side] - turned[1, ..., side:]) * scale
    imag_part = (turned[0, ..., side:] + turned[1, ..., :side]) * scale
    series = jnp.stack([real_part, imag_part], 1)
    return series, jnp.max(real_part * real_part + imag_part * imag_part, axis=0)


def local(device_count, strain, inv_asd, spectra, cutoff):
    rows, side = strain.shape
    templ_count = spectra.shape[1]
    tiles_fit = rows % 16 == 0 and 2 * templ_count * rows == 128 and side % 128 == 0
    vmem = pl.BlockSpec(memory_space=pltpu.VMEM)
    chips = device_count // 2
    groups = [[2 * chip + core for chip in range(chips)] for core in range(2)]
    copies = jnp.broadcast_to(strain.astype(jnp.bfloat16)[None], (chips, rows, side))
    own = lax.all_to_all(copies, "freq", 0, 0, tiled=True, axis_index_groups=groups).reshape(-1, side)
    turns, table = jnp.asarray(device_tables(side, rows)), jnp.asarray(transform_table(side))
    if tiles_fit:
        twist, forward, table = pl.pallas_call(
            prepare_kernel,
            out_shape=(
                jax.ShapeDtypeStruct((2, rows, side), jnp.float32),
                jax.ShapeDtypeStruct((4 * rows, side), jnp.bfloat16),
                jax.ShapeDtypeStruct(table.shape, jnp.bfloat16),
            ),
            in_specs=[vmem, pl.BlockSpec(memory_space=pl.ANY)],
            out_specs=(vmem, vmem, vmem),
            scratch_shapes=[pltpu.SemaphoreType.DMA(())],
            compiler_params=pltpu.CompilerParams(vmem_limit_bytes=VMEM_LIMIT),
            cost_estimate=pl.CostEstimate(flops=0, bytes_accessed=16 * table.size, transcendentals=0),
        )(turns, table)
    else:
        twist, forward, table = prepare_plain(turns, table, rows)
    keep = jnp.arange(BAND, dtype=jnp.int32)[None, :] < cutoff[:, None]
    kept = jnp.where(keep[:, None, None], jnp.transpose(spectra[..., :BAND], (1, 2, 0, 3)), 0)
    ready = (twist, forward, table, inv_asd[:, :BAND], kept)
    own, ready = lax.optimization_barrier((own, ready))
    table = ready[2]
    other = lax.ppermute(own, "freq", [(i, i ^ 1) for i in range(device_count)])
    args = (own, other) + ready
    if tiles_fit:
        outgoing = pl.pallas_call(
            middle_kernel,
            out_shape=jax.ShapeDtypeStruct((device_count, rows, 128), jnp.bfloat16),
            in_specs=[vmem] * len(args),
            out_specs=vmem,
            compiler_params=pltpu.CompilerParams(vmem_limit_bytes=VMEM_LIMIT),
        )(*args)
    else:
        outgoing = middle_plain(*args)
    received = lax.all_to_all(outgoing, "freq", 0, 0, tiled=True).reshape(side, -1)
    if tiles_fit:
        series, peak = pl.pallas_call(
            last_kernel,
            out_shape=(
                jax.ShapeDtypeStruct((templ_count, 2, rows, side), jnp.float32),
                jax.ShapeDtypeStruct((rows, side), jnp.float32),
            ),
            in_specs=[vmem] * 2,
            out_specs=(vmem, vmem),
            compiler_params=pltpu.CompilerParams(vmem_limit_bytes=VMEM_LIMIT),
        )(received, table)
    else:
        series, peak = last_plain(received, table, templ_count, rows)
    return series, lax.pmax(peak, "tmpl")


def solution(mesh):
    in_specs = (P("freq", None), P("freq", None), P("freq", "tmpl", None, None), P("tmpl"))
    out_specs = (P("tmpl", None, "freq", None), P("freq", None))
    return jax.shard_map(
        functools.partial(local, mesh.shape["freq"]),
        mesh=mesh,
        in_specs=in_specs,
        out_specs=out_specs,
        check_vma=False,
    )
```

```python
import functools

import jax
import jax.numpy as jnp
import ml_dtypes
import numpy as np
from jax import lax
from jax.experimental import pallas as pl
from jax.experimental.pallas import tpu as pltpu
from jax.sharding import PartitionSpec as P

BAND = 256
CORES = 2
INNER = 4
VMEM_LIMIT = 16 << 20


def angles(left, right, modulus):
    return 2.0 * np.pi / modulus * (left[:, None] * right[None, :] % modulus)


def split(table):
    high = table.astype(ml_dtypes.bfloat16)
    low = (table - high.astype(np.float64)).astype(ml_dtypes.bfloat16)
    return high, low


def rows_of(devices, rows):
    return (np.asarray(devices)[:, None] * rows + np.arange(rows)).reshape(-1)


def device_tables(count, rows, side):
    outer = count // (INNER * CORES)
    positions = np.arange(side)
    forward, twist = [], []
    for device in range(count):
        wanted = rows_of([device ^ (INNER * CORES * j) for j in range(outer)], rows)
        held = rows_of([device ^ core ^ (CORES * m) for core in range(CORES) for m in range(INNER)], rows)
        angle = angles(wanted, held, side)
        forward.append(np.concatenate(split(np.concatenate([np.cos(angle), -np.sin(angle)]))))
        angle = angles(wanted, positions, side * side)
        twist.append(np.stack([np.cos(angle), np.sin(angle)]))
    return np.stack(forward), np.stack(twist).astype(np.float32)


def transform_table(side):
    angle = angles(np.arange(side), np.arange(side), side)
    cos_high, cos_low = split(np.cos(angle))
    sin_high, sin_low = split(np.sin(angle))
    return np.concatenate([cos_high, sin_high, cos_low[:, :BAND], sin_low[:, :BAND]], 1)


def dot(left, right):
    return jnp.dot(left, right, preferred_element_type=jnp.float32)


def halves(value):
    high = value.astype(jnp.bfloat16)
    return high, (value - high.astype(jnp.float32)).astype(jnp.bfloat16)


def partial_spectrum(blocks, forward, twist, table):
    _, wanted, side = twist.shape
    high, low = halves(jnp.concatenate(blocks, 0))
    both = dot(forward, high)
    first = both[: 2 * wanted] + both[2 * wanted :] + dot(forward[: 2 * wanted], low)
    real, imag = first[:wanted], first[wanted:]
    turned = jnp.concatenate([real * twist[0] + imag * twist[1], imag * twist[0] - real * twist[1]], 0)
    high, low = halves(turned)
    by_part = []
    for part in range(2):
        both = dot(jnp.concatenate([high, low], 0), table[:, part * side : part * side + BAND])
        rest = dot(high, table[:, 2 * side + part * BAND : 2 * side + (part + 1) * BAND])
        by_part.append(both[: 2 * wanted] + both[2 * wanted :] + rest)
    by_cos, by_sin = by_part
    return by_cos[:wanted] + by_sin[wanted:], by_cos[wanted:] - by_sin[:wanted]


def sections(parts, asd, keep, spectra, twist_cos, twist_sin, table):
    templ_count, _, rows, _ = spectra.shape
    side = twist_cos.shape[1]
    white = functools.reduce(jnp.add, parts)
    white_real, white_imag = white[:rows] * asd, white[rows:] * asd
    product = []
    for part in range(2):
        for templ in range(templ_count):
            spec_real = spectra[templ, 0].astype(jnp.float32)
            spec_imag = spectra[templ, 1].astype(jnp.float32)
            if part == 0:
                value = white_real * spec_real + white_imag * spec_imag
            else:
                value = white_imag * spec_real - white_real * spec_imag
            product.append(jnp.where(keep[templ : templ + 1] > 0, value, 0.0).astype(jnp.bfloat16))
    turned = dot(jnp.concatenate(product, 0), table[:BAND, : 2 * side])
    group = templ_count * rows
    real_part = turned[:group, :side] - turned[group:, side:]
    imag_part = turned[:group, side:] + turned[group:, :side]
    result = []
    for part in range(2):
        for templ in range(templ_count):
            here = slice(templ * rows, (templ + 1) * rows)
            if part == 0:
                result.append(real_part[here] * twist_cos - imag_part[here] * twist_sin)
            else:
                result.append(real_part[here] * twist_sin + imag_part[here] * twist_cos)
    return result


def last_stage(received, table, templ_count):
    side = received.shape[0]
    scale = 1.0 / (side * side)
    turned = lax.dot_general(received, table, (((0,), (0,)), ((), ())), preferred_element_type=jnp.float32)
    group = turned.shape[0] // 2
    real_part = (turned[:group, :side] - turned[group:, side:]) * scale
    imag_part = (turned[:group, side:] + turned[group:, :side]) * scale
    return real_part, imag_part


def spread(slots, rows):
    count = len(slots)
    lane = lax.broadcasted_iota(jnp.int32, slots[0].shape, 1)
    lanes = slots[0].shape[1]
    bit = 1
    while bit < count:
        step = rows * bit
        keep = (lane // step) % 2 == 0
        after = list(slots)
        for low in range(count):
            if low & bit:
                continue
            high = low | bit
            after[low] = jnp.where(keep, slots[low], pltpu.roll(slots[high], step, 1))
            after[high] = jnp.where(keep, pltpu.roll(slots[low], lanes - step, 1), slots[high])
        slots = after
        bit *= 2
    return slots


def prepare_kernel(
    forwards, twists, table, strain, inv_asd, cutoff, forward, twist, table_out, strain_out, asd, keep, limits, arrived
):
    device = lax.axis_index("freq")
    moves = (
        (cutoff, limits),
        (strain, strain_out),
        (forwards.at[device], forward),
        (twists.at[device], twist),
        (inv_asd.at[:, :BAND], asd),
        (table, table_out),
    )
    copies = [pltpu.make_async_copy(source, target, arrived.at[i]) for i, (source, target) in enumerate(moves)]
    for copy in copies:
        copy.start()
    copies[0].wait()
    band = lax.broadcasted_iota(jnp.int32, (1, BAND), 1)
    for templ in range(keep.shape[0]):
        keep[templ : templ + 1, :] = jnp.where(band < limits[templ], 1.0, 0.0)
    for copy in copies[1:]:
        copy.wait()


def spectrum_kernel(*refs):
    inputs = INNER * CORES + 3
    (*blocks, forward, twist, table), outs = refs[:inputs], refs[inputs:]
    real, imag = partial_spectrum([block[...] for block in blocks], forward[...], twist, table)
    rows = outs[0].shape[0] // 2
    for m, out in enumerate(outs):
        out[:rows] = real[m * rows : (m + 1) * rows]
        out[rows:] = imag[m * rows : (m + 1) * rows]


def section_kernel(*refs):
    *parts, asd, keep, spectra, twist, table, out = refs
    rows = asd.shape[0]
    slots = sections(
        [part[...] for part in parts], asd[...], keep[...], spectra, twist[0, :rows], twist[1, :rows], table
    )
    for start in range(0, twist.shape[2], 128):
        pieces = spread([slot[:, start : start + 128] for slot in slots], rows)
        for place, piece in enumerate(pieces):
            out[start // rows + place] = piece.astype(jnp.bfloat16)


def last_kernel(received, table, series, peak):
    templ_count, _, rows, side = series.shape
    real_part, imag_part = last_stage(received[...], table[:, : 2 * side], templ_count)
    power = real_part * real_part + imag_part * imag_part
    best = power[:rows]
    for templ in range(templ_count):
        here = slice(templ * rows, (templ + 1) * rows)
        series[templ, 0] = real_part[here]
        series[templ, 1] = imag_part[here]
        best = jnp.maximum(best, power[here])
    peak[...] = best


def local(device_count, strain, inv_asd, spectra, cutoff):
    rows, side = strain.shape
    templ_count = spectra.shape[1]
    outer = device_count // (INNER * CORES)
    forwards, twists = (jnp.asarray(x) for x in device_tables(device_count, rows, side))
    table = jnp.asarray(transform_table(side))
    tiles_fit = rows % 16 == 0 and 2 * templ_count * rows == 128 and side % 128 == 0
    params = pltpu.CompilerParams(vmem_limit_bytes=VMEM_LIMIT)
    vmem = pl.BlockSpec(memory_space=pltpu.VMEM)
    hbm = pl.BlockSpec(memory_space=pltpu.HBM)

    def swap(value, distance):
        return lax.ppermute(value, "freq", [(i, i ^ distance) for i in range(device_count)])

    held = [None] * INNER
    for m in (3, 2, 1):
        held[m] = swap(strain, CORES * m)
    if tiles_fit:
        results = [
            pltpu.VMEM(forwards.shape[1:], jnp.bfloat16),
            pltpu.VMEM(twists.shape[1:], jnp.float32),
            pltpu.VMEM(table.shape, jnp.bfloat16),
            pltpu.VMEM(strain.shape, jnp.float32),
            pltpu.VMEM((rows, BAND), jnp.float32),
            pltpu.VMEM((templ_count, BAND), jnp.float32),
        ]
        sources = (forwards, twists, table, strain, inv_asd, cutoff)
        forward, twist, table, mine, asd, keep = pl.pallas_call(
            prepare_kernel,
            out_shape=results,
            in_specs=[hbm] * 6,
            out_specs=[vmem] * 6,
            scratch_shapes=[pltpu.SMEM(cutoff.shape, jnp.int32), pltpu.SemaphoreType.DMA((6,))],
            compiler_params=params,
            cost_estimate=pl.CostEstimate(flops=0, bytes_accessed=4 * table.size, transcendentals=0),
        )(*[pltpu.with_memory_space_constraint(source, pltpu.HBM) for source in sources])
    else:
        device = lax.axis_index("freq")
        forward, twist, mine, asd = forwards[device], twists[device], strain, inv_asd[:, :BAND]
        keep = (jnp.arange(BAND, dtype=jnp.int32)[None, :] < cutoff[:, None]).astype(jnp.float32)
    by_templ = jnp.transpose(spectra[..., :BAND], (1, 2, 0, 3))
    held[0] = mine
    held[1], forward, twist, table, asd, keep = lax.optimization_barrier((held[1], forward, twist, table, asd, keep))
    blocks = held + [swap(strain if j == 0 else block, 1) for j, block in enumerate(held)]
    if tiles_fit:
        parts = pl.pallas_call(
            spectrum_kernel,
            out_shape=[jax.ShapeDtypeStruct((2 * rows, BAND), jnp.float32)] * outer,
            in_specs=[vmem] * (len(blocks) + 3),
            out_specs=[vmem] * outer,
            compiler_params=params,
        )(*blocks, forward, twist, table)
    else:
        real, imag = partial_spectrum(blocks, forward, twist, table)
        parts = [jnp.concatenate([x[m * rows : (m + 1) * rows] for x in (real, imag)], 0) for m in range(outer)]
    parts, by_templ = lax.optimization_barrier((list(parts), by_templ))
    parts = [parts[0]] + [swap(parts[j], INNER * CORES * j) for j in (3, 1, 2)]
    if tiles_fit:
        outgoing = pl.pallas_call(
            section_kernel,
            out_shape=jax.ShapeDtypeStruct((device_count, rows, 128), jnp.bfloat16),
            in_specs=[vmem] * (outer + 5),
            out_specs=vmem,
            compiler_params=params,
        )(*parts, asd, keep, by_templ, twist, table)
    else:
        slots = sections(parts, asd, keep, by_templ, twist[0, :rows], twist[1, :rows], table)
        slots = jnp.stack(slots).astype(jnp.bfloat16).reshape(2 * templ_count, rows, device_count, rows)
        outgoing = jnp.transpose(slots, (2, 1, 0, 3)).reshape(device_count, rows, -1)
    received = lax.all_to_all(outgoing, "freq", 0, 0, tiled=True).reshape(side, -1)
    if tiles_fit:
        series, peak = pl.pallas_call(
            last_kernel,
            out_shape=(
                jax.ShapeDtypeStruct((templ_count, 2, rows, side), jnp.float32),
                jax.ShapeDtypeStruct((rows, side), jnp.float32),
            ),
            in_specs=[vmem] * 2,
            out_specs=(vmem, vmem),
            compiler_params=params,
        )(received, table)
    else:
        both = jnp.stack(last_stage(received, table[:, : 2 * side], templ_count))
        series = jnp.transpose(both.reshape(2, templ_count, rows, side), (1, 0, 2, 3))
        peak = jnp.max(series[:, 0] ** 2 + series[:, 1] ** 2, axis=0)
    return series, lax.pmax(peak, "tmpl")


def solution(mesh):
    in_specs = (P("freq", None), P("freq", None), P("freq", "tmpl", None, None), P("tmpl"))
    out_specs = (P("tmpl", None, "freq", None), P("freq", None))
    return jax.shard_map(
        functools.partial(local, mesh.shape["freq"]),
        mesh=mesh,
        in_specs=in_specs,
        out_specs=out_specs,
        check_vma=False,
    )
```

```python
import functools

import jax
import jax.numpy as jnp
import ml_dtypes
import numpy as np
from jax import lax
from jax.experimental import pallas as pl
from jax.experimental.pallas import tpu as pltpu
from jax.sharding import PartitionSpec as P

BAND = 256
CORES = 2
INNER = 4
LANES = 128
VMEM_LIMIT = 16 << 20


def angles(left, right, modulus):
    return 2.0 * np.pi / modulus * (left[:, None] * right[None, :] % modulus)


def split(table):
    high = table.astype(ml_dtypes.bfloat16)
    low = (table - high.astype(np.float64)).astype(ml_dtypes.bfloat16)
    return high, low


def rows_of(devices, rows):
    return (np.asarray(devices)[:, None] * rows + np.arange(rows)).reshape(-1)


def plane(device, step):
    return device ^ (CORES * step ^ 1 if step else 0)


def line(device, step):
    return device ^ (INNER * CORES * step ^ 1 if step else 0)


def device_tables(count, rows, side):
    outer = count // (INNER * CORES)
    positions = np.arange(side)
    forward, twist = [], []
    for device in range(count):
        wanted = rows_of([line(device, step) for step in range(outer)], rows)
        held = rows_of([plane(device ^ core, step) for core in range(CORES) for step in range(INNER)], rows)
        angle = angles(wanted, held, side)
        forward.append(np.concatenate(split(np.concatenate([np.cos(angle), -np.sin(angle)]))))
        angle = angles(wanted, positions, side * side)
        twist.append(np.stack([np.cos(angle), np.sin(angle)]))
    return np.stack(forward), np.stack(twist).astype(np.float32)


def transform_table(side):
    angle = angles(np.arange(side), np.arange(side), side)
    cos_high, cos_low = split(np.cos(angle))
    sin_high, sin_low = split(np.sin(angle))
    columns = []
    for cos_part, sin_part, width in ((cos_high, sin_high, side), (cos_low, sin_low, BAND)):
        for start in range(0, width, LANES):
            columns += [x[:, start : start + LANES] for x in (cos_part, sin_part)]
    return np.concatenate(columns, 1)


def dot(left, right):
    return jnp.dot(left, right, preferred_element_type=jnp.float32)


def halves(value):
    high = value.astype(jnp.bfloat16)
    return high, (value - high.astype(jnp.float32)).astype(jnp.bfloat16)


def turns(value):
    starts = range(0, value.shape[1], 2 * LANES)
    return tuple(
        jnp.concatenate([value[:, start + part : start + part + LANES] for start in starts], 1) for part in (0, LANES)
    )


def partial_spectrum(blocks, forward, twist, table):
    _, wanted, side = twist.shape
    high, low = halves(jnp.concatenate(blocks, 0))
    both = dot(forward, high)
    first = both[: 2 * wanted] + both[2 * wanted :] + dot(forward[: 2 * wanted], low)
    real, imag = first[:wanted], first[wanted:]
    turned = jnp.concatenate([real * twist[0] + imag * twist[1], imag * twist[0] - real * twist[1]], 0)
    high, low = halves(turned)
    both = dot(jnp.concatenate([high, low], 0), table[:, : 2 * BAND])
    second = both[: 2 * wanted] + both[2 * wanted :] + dot(high, table[:, 2 * side :])
    by_cos, by_sin = turns(second)
    return by_cos[:wanted] + by_sin[wanted:], by_cos[wanted:] - by_sin[:wanted]


def products(parts, asd, keep, spectra):
    templ_count, _, rows, _ = spectra.shape
    white = functools.reduce(jnp.add, parts)
    white_real, white_imag = white[:rows] * asd, white[rows:] * asd
    result = []
    for part in range(2):
        for templ in range(templ_count):
            spec_real = spectra[templ, 0].astype(jnp.float32)
            spec_imag = spectra[templ, 1].astype(jnp.float32)
            if part == 0:
                value = white_real * spec_real + white_imag * spec_imag
            else:
                value = white_imag * spec_real - white_real * spec_imag
            result.append(jnp.where(keep[templ : templ + 1] > 0, value, 0.0).astype(jnp.bfloat16))
    return jnp.concatenate(result, 0)


def section(product, table, twist_cos, twist_sin):
    rows = twist_cos.shape[0]
    group = product.shape[0] // 2
    by_cos, by_sin = turns(dot(product, table))
    real_part = by_cos[:group] - by_sin[group:]
    imag_part = by_sin[:group] + by_cos[group:]
    result = []
    for part in range(2):
        for start in range(0, group, rows):
            here = slice(start, start + rows)
            if part == 0:
                result.append(real_part[here] * twist_cos - imag_part[here] * twist_sin)
            else:
                result.append(real_part[here] * twist_sin + imag_part[here] * twist_cos)
    return result


def last_stage(received, table, total):
    turned = lax.dot_general(received, table, (((0,), (0,)), ((), ())), preferred_element_type=jnp.float32)
    by_cos, by_sin = turns(turned)
    group = turned.shape[0] // 2
    return (by_cos[:group] - by_sin[group:]) * (1.0 / total), (by_sin[:group] + by_cos[group:]) * (1.0 / total)


def spread(slots, rows):
    count = len(slots)
    lane = lax.broadcasted_iota(jnp.int32, slots[0].shape, 1)
    lanes = slots[0].shape[1]
    bit = 1
    while bit < count:
        step = rows * bit
        keep = (lane // step) % 2 == 0
        after = list(slots)
        for low in range(count):
            if low & bit:
                continue
            high = low | bit
            after[low] = jnp.where(keep, slots[low], pltpu.roll(slots[high], step, 1))
            after[high] = jnp.where(keep, pltpu.roll(slots[low], lanes - step, 1), slots[high])
        slots = after
        bit *= 2
    return slots


def prepare_kernel(
    forwards, twists, table, strain, inv_asd, cutoff, forward, twist, table_out, strain_out, asd, keep, limits, arrived
):
    device = lax.axis_index("freq")
    moves = (
        (cutoff, limits),
        (strain, strain_out),
        (forwards.at[device], forward),
        (twists.at[device], twist),
        (inv_asd.at[:, :BAND], asd),
        (table, table_out),
    )
    copies = [pltpu.make_async_copy(source, target, arrived.at[i]) for i, (source, target) in enumerate(moves)]
    for copy in copies:
        copy.start()
    copies[0].wait()
    band = lax.broadcasted_iota(jnp.int32, (1, BAND), 1)
    for templ in range(keep.shape[0]):
        keep[templ : templ + 1, :] = jnp.where(band < limits[templ], 1.0, 0.0)
    for copy in copies[1:]:
        copy.wait()


def spectrum_kernel(*refs):
    inputs = INNER * CORES + 3
    (*blocks, forward, twist, table), outs = refs[:inputs], refs[inputs:]
    real, imag = partial_spectrum([block[...] for block in blocks], forward[...], twist, table)
    rows = outs[0].shape[0] // 2
    for m, out in enumerate(outs):
        out[:rows] = real[m * rows : (m + 1) * rows]
        out[rows:] = imag[m * rows : (m + 1) * rows]


def section_kernel(*refs):
    *parts, asd, keep, spectra, twist, table, out = refs
    rows = asd.shape[0]
    product = products([part[...] for part in parts], asd[...], keep[...], spectra)
    for start in range(0, twist.shape[2], LANES):
        columns = slice(start, start + LANES)
        slots = section(
            product, table[:BAND, 2 * start : 2 * (start + LANES)], twist[0, :rows, columns], twist[1, :rows, columns]
        )
        for place, piece in enumerate(spread(slots, rows)):
            out[start // rows + place] = piece.astype(jnp.bfloat16)


def last_kernel(received, table, series, peak):
    templ_count, _, rows, side = series.shape
    values = received[...]
    for start in range(0, side, LANES):
        columns = slice(start, start + LANES)
        real_part, imag_part = last_stage(values, table[:, 2 * start : 2 * (start + LANES)], side * side)
        power = real_part * real_part + imag_part * imag_part
        best = power[:rows]
        for templ in range(templ_count):
            here = slice(templ * rows, (templ + 1) * rows)
            series[templ, 0, :, columns] = real_part[here]
            series[templ, 1, :, columns] = imag_part[here]
            best = jnp.maximum(best, power[here])
        peak[:, columns] = best

def local(device_count, strain, inv_asd, spectra, cutoff):
    rows, side = strain.shape
    templ_count = spectra.shape[1]
    outer = device_count // (INNER * CORES)
    forwards, twists = (jnp.asarray(x) for x in device_tables(device_count, rows, side))
    table = jnp.asarray(transform_table(side))
    tiles_fit = rows % 16 == 0 and 2 * templ_count * rows == 128 and side % 128 == 0
    params = pltpu.CompilerParams(vmem_limit_bytes=VMEM_LIMIT)
    vmem = pl.BlockSpec(memory_space=pltpu.VMEM)
    hbm = pl.BlockSpec(memory_space=pltpu.HBM)

    def exchange(value, partner):
        return lax.ppermute(value, "freq", [(i, partner(i)) for i in range(device_count)])

    held = [strain] + [exchange(strain, functools.partial(plane, step=step)) for step in range(1, INNER)]
    if tiles_fit:
        results = [
            pltpu.VMEM(forwards.shape[1:], jnp.bfloat16),
            pltpu.VMEM(twists.shape[1:], jnp.float32),
            pltpu.VMEM(table.shape, jnp.bfloat16),
            pltpu.VMEM(strain.shape, jnp.float32),
            pltpu.VMEM((rows, BAND), jnp.float32),
            pltpu.VMEM((templ_count, BAND), jnp.float32),
        ]
        sources = (forwards, twists, table, strain, inv_asd, cutoff)
        forward, twist, table, mine, asd, keep = pl.pallas_call(
            prepare_kernel,
            out_shape=results,
            in_specs=[hbm] * 6,
            out_specs=[vmem] * 6,
            scratch_shapes=[pltpu.SMEM(cutoff.shape, jnp.int32), pltpu.SemaphoreType.DMA((6,))],
            compiler_params=params,
            cost_estimate=pl.CostEstimate(flops=0, bytes_accessed=4 * table.size, transcendentals=0),
        )(*[pltpu.with_memory_space_constraint(source, pltpu.HBM) for source in sources])
    else:
        device = lax.axis_index("freq")
        forward, twist, mine, asd = forwards[device], twists[device], strain, inv_asd[:, :BAND]
        keep = (jnp.arange(BAND, dtype=jnp.int32)[None, :] < cutoff[:, None]).astype(jnp.float32)
    by_templ = jnp.transpose(spectra[..., :BAND], (1, 2, 0, 3))
    held[0] = mine
    held[1], forward, twist, table, asd, keep = lax.optimization_barrier((held[1], forward, twist, table, asd, keep))
    blocks = held + [exchange(block, lambda i: i ^ 1) for block in [strain] + held[1:]]
    if tiles_fit:
        parts = pl.pallas_call(
            spectrum_kernel,
            out_shape=[jax.ShapeDtypeStruct((2 * rows, BAND), jnp.float32)] * outer,
            in_specs=[vmem] * (len(blocks) + 3),
            out_specs=[vmem] * outer,
            compiler_params=params,
        )(*blocks, forward, twist, table)
    else:
        real, imag = partial_spectrum(blocks, forward, twist, table)
        parts = [jnp.concatenate([x[m * rows : (m + 1) * rows] for x in (real, imag)], 0) for m in range(outer)]
    parts, by_templ = lax.optimization_barrier((list(parts), by_templ))
    received = [exchange(parts[step], functools.partial(line, step=step)) for step in reversed(range(1, outer))]
    parts = parts[:1] + received
    if tiles_fit:
        outgoing = pl.pallas_call(
            section_kernel,
            out_shape=jax.ShapeDtypeStruct((device_count, rows, 128), jnp.bfloat16),
            in_specs=[vmem] * (outer + 5),
            out_specs=vmem,
            compiler_params=params,
        )(*parts, asd, keep, by_templ, twist, table)
    else:
        product = products(parts, asd, keep, by_templ)
        slots = section(product, table[:BAND, : 2 * side], twist[0, :rows], twist[1, :rows])
        slots = jnp.stack(slots).astype(jnp.bfloat16).reshape(2 * templ_count, rows, device_count, rows)
        outgoing = jnp.transpose(slots, (2, 1, 0, 3)).reshape(device_count, rows, -1)
    received = lax.all_to_all(outgoing, "freq", 0, 0, tiled=True).reshape(side, -1)
    if tiles_fit:
        series, peak = pl.pallas_call(
            last_kernel,
            out_shape=(
                jax.ShapeDtypeStruct((templ_count, 2, rows, side), jnp.float32),
                jax.ShapeDtypeStruct((rows, side), jnp.float32),
            ),
            in_specs=[vmem] * 2,
            out_specs=(vmem, vmem),
            compiler_params=params,
        )(received, table)
    else:
        both = jnp.stack(last_stage(received, table[:, : 2 * side], side * side))
        series = jnp.transpose(both.reshape(2, templ_count, rows, side), (1, 0, 2, 3))
        peak = jnp.max(series[:, 0] ** 2 + series[:, 1] ** 2, axis=0)
    return series, lax.pmax(peak, "tmpl")


def solution(mesh):
    in_specs = (P("freq", None), P("freq", None), P("freq", "tmpl", None, None), P("tmpl"))
    out_specs = (P("tmpl", None, "freq", None), P("freq", None))
    return jax.shard_map(
        functools.partial(local, mesh.shape["freq"]),
        mesh=mesh,
        in_specs=in_specs,
        out_specs=out_specs,
        check_vma=False,
    )
```

```python
import functools

import jax
import jax.numpy as jnp
import ml_dtypes
import numpy as np
from jax import lax
from jax.experimental import pallas as pl
from jax.experimental.pallas import tpu as pltpu
from jax.sharding import PartitionSpec as P

BAND = 256
CORES = 2
INNER = 4
LANES = 128
VMEM_LIMIT = 16 << 20


def angles(left, right, modulus):
    return 2.0 * np.pi / modulus * (left[:, None] * right[None, :] % modulus)


def split(table):
    high = table.astype(ml_dtypes.bfloat16)
    low = (table - high.astype(np.float64)).astype(ml_dtypes.bfloat16)
    return high, low


def rows_of(devices, rows):
    return (np.asarray(devices)[:, None] * rows + np.arange(rows)).reshape(-1)


def across(device):
    return device ^ (INNER - 1) * CORES ^ 1


def beside(device):
    chip = device // CORES
    return device ^ CORES * (1 + (chip + chip // 2 + device) % 2) ^ 1


def held_by(device):
    result = [device, device ^ 1]
    for here in (device, device ^ 1):
        result += [beside(here), beside(here) ^ 1, across(here)]
    return result


def line(device, step):
    return device ^ (INNER * CORES * step ^ 1 if step else 0)


def device_tables(count, rows, side):
    outer = count // (INNER * CORES)
    positions = np.arange(side)
    forward, twist = [], []
    for device in range(count):
        wanted = rows_of([line(device, step) for step in range(outer)], rows)
        held = rows_of(held_by(device), rows)
        angle = angles(wanted, held, side)
        forward.append(np.concatenate(split(np.concatenate([np.cos(angle), -np.sin(angle)]))))
        angle = angles(wanted, positions, side * side)
        twist.append(np.stack([np.cos(angle), np.sin(angle)]))
    return np.stack(forward), np.stack(twist).astype(np.float32)


def transform_table(side):
    angle = angles(np.arange(side), np.arange(side), side)
    cos_high, cos_low = split(np.cos(angle))
    sin_high, sin_low = split(np.sin(angle))
    columns = []
    for cos_part, sin_part, width in ((cos_high, sin_high, side), (cos_low, sin_low, BAND)):
        for start in range(0, width, LANES):
            columns += [x[:, start : start + LANES] for x in (cos_part, sin_part)]
    return np.concatenate(columns, 1)


def dot(left, right):
    return jnp.dot(left, right, preferred_element_type=jnp.float32)


def halves(value):
    high = value.astype(jnp.bfloat16)
    return high, (value - high.astype(jnp.float32)).astype(jnp.bfloat16)


def turns(value):
    starts = range(0, value.shape[1], 2 * LANES)
    return tuple(
        jnp.concatenate([value[:, start + part : start + part + LANES] for start in starts], 1) for part in (0, LANES)
    )


def partial_spectrum(blocks, forward, twist, table):
    _, wanted, side = twist.shape
    high, low = halves(jnp.concatenate(blocks, 0))
    both = dot(forward, high)
    first = both[: 2 * wanted] + both[2 * wanted :] + dot(forward[: 2 * wanted], low)
    real, imag = first[:wanted], first[wanted:]
    turned = jnp.concatenate([real * twist[0] + imag * twist[1], imag * twist[0] - real * twist[1]], 0)
    high, low = halves(turned)
    both = dot(jnp.concatenate([high, low], 0), table[:, : 2 * BAND])
    second = both[: 2 * wanted] + both[2 * wanted :] + dot(high, table[:, 2 * side :])
    by_cos, by_sin = turns(second)
    return by_cos[:wanted] + by_sin[wanted:], by_cos[wanted:] - by_sin[:wanted]


def products(parts, asd, keep, spectra):
    templ_count, _, rows, _ = spectra.shape
    white = functools.reduce(jnp.add, parts)
    white_real, white_imag = white[:rows] * asd, white[rows:] * asd
    result = []
    for part in range(2):
        for templ in range(templ_count):
            spec_real = spectra[templ, 0].astype(jnp.float32)
            spec_imag = spectra[templ, 1].astype(jnp.float32)
            if part == 0:
                value = white_real * spec_real + white_imag * spec_imag
            else:
                value = white_imag * spec_real - white_real * spec_imag
            result.append(jnp.where(keep[templ : templ + 1] > 0, value, 0.0).astype(jnp.bfloat16))
    return jnp.concatenate(result, 0)


def section(product, table, twist_cos, twist_sin):
    rows = twist_cos.shape[0]
    group = product.shape[0] // 2
    by_cos, by_sin = turns(dot(product, table))
    real_part = by_cos[:group] - by_sin[group:]
    imag_part = by_sin[:group] + by_cos[group:]
    result = []
    for part in range(2):
        for start in range(0, group, rows):
            here = slice(start, start + rows)
            if part == 0:
                result.append(real_part[here] * twist_cos - imag_part[here] * twist_sin)
            else:
                result.append(real_part[here] * twist_sin + imag_part[here] * twist_cos)
    return result


def last_stage(received, table, total):
    turned = lax.dot_general(received, table, (((0,), (0,)), ((), ())), preferred_element_type=jnp.float32)
    by_cos, by_sin = turns(turned)
    group = turned.shape[0] // 2
    return (by_cos[:group] - by_sin[group:]) * (1.0 / total), (by_sin[:group] + by_cos[group:]) * (1.0 / total)


def spread(slots, rows):
    count = len(slots)
    lane = lax.broadcasted_iota(jnp.int32, slots[0].shape, 1)
    lanes = slots[0].shape[1]
    bit = 1
    while bit < count:
        step = rows * bit
        keep = (lane // step) % 2 == 0
        after = list(slots)
        for low in range(count):
            if low & bit:
                continue
            high = low | bit
            after[low] = jnp.where(keep, slots[low], pltpu.roll(slots[high], step, 1))
            after[high] = jnp.where(keep, pltpu.roll(slots[low], lanes - step, 1), slots[high])
        slots = after
        bit *= 2
    return slots


def prepare_kernel(
    forwards, twists, table, strain, inv_asd, cutoff, forward, twist, table_out, strain_out, asd, keep, limits, arrived
):
    device = lax.axis_index("freq")
    moves = (
        (cutoff, limits),
        (strain, strain_out),
        (forwards.at[device], forward),
        (twists.at[device], twist),
        (inv_asd.at[:, :BAND], asd),
        (table, table_out),
    )
    copies = [pltpu.make_async_copy(source, target, arrived.at[i]) for i, (source, target) in enumerate(moves)]
    for copy in copies:
        copy.start()
    copies[0].wait()
    band = lax.broadcasted_iota(jnp.int32, (1, BAND), 1)
    for templ in range(keep.shape[0]):
        keep[templ : templ + 1, :] = jnp.where(band < limits[templ], 1.0, 0.0)
    for copy in copies[1:]:
        copy.wait()


def spectrum_kernel(*refs):
    inputs = INNER * CORES + 3
    (*blocks, forward, twist, table), outs = refs[:inputs], refs[inputs:]
    real, imag = partial_spectrum([block[...] for block in blocks], forward[...], twist, table)
    rows = outs[0].shape[0] // 2
    for m, out in enumerate(outs):
        out[:rows] = real[m * rows : (m + 1) * rows]
        out[rows:] = imag[m * rows : (m + 1) * rows]


def section_kernel(*refs):
    *parts, asd, keep, spectra, twist, table, out = refs
    rows = asd.shape[0]
    product = products([part[...] for part in parts], asd[...], keep[...], spectra)
    for start in range(0, twist.shape[2], LANES):
        columns = slice(start, start + LANES)
        slots = section(
            product, table[:BAND, 2 * start : 2 * (start + LANES)], twist[0, :rows, columns], twist[1, :rows, columns]
        )
        for place, piece in enumerate(spread(slots, rows)):
            out[start // rows + place] = piece.astype(jnp.bfloat16)


def last_kernel(received, table, series, peak):
    templ_count, _, rows, side = series.shape
    values = received[...]
    for start in range(0, side, LANES):
        columns = slice(start, start + LANES)
        real_part, imag_part = last_stage(values, table[:, 2 * start : 2 * (start + LANES)], side * side)
        power = real_part * real_part + imag_part * imag_part
        best = power[:rows]
        for templ in range(templ_count):
            here = slice(templ * rows, (templ + 1) * rows)
            series[templ, 0, :, columns] = real_part[here]
            series[templ, 1, :, columns] = imag_part[here]
            best = jnp.maximum(best, power[here])
        peak[:, columns] = best


def local(device_count, strain, inv_asd, spectra, cutoff):
    rows, side = strain.shape
    templ_count = spectra.shape[1]
    outer = device_count // (INNER * CORES)
    forwards, twists = (jnp.asarray(x) for x in device_tables(device_count, rows, side))
    table = jnp.asarray(transform_table(side))
    tiles_fit = rows % 16 == 0 and 2 * templ_count * rows == 128 and side % 128 == 0
    params = pltpu.CompilerParams(vmem_limit_bytes=VMEM_LIMIT)
    vmem = pl.BlockSpec(memory_space=pltpu.VMEM)
    hbm = pl.BlockSpec(memory_space=pltpu.HBM)

    def exchange(value, partner):
        return lax.ppermute(value, "freq", [(i, partner(i)) for i in range(device_count)])

    other = exchange(strain, lambda i: i ^ 1)
    first = exchange(strain, beside)
    second = exchange(other, beside)
    single = exchange(strain, across)
    if tiles_fit:
        results = [
            pltpu.VMEM(forwards.shape[1:], jnp.bfloat16),
            pltpu.VMEM(twists.shape[1:], jnp.float32),
            pltpu.VMEM(table.shape, jnp.bfloat16),
            pltpu.VMEM(strain.shape, jnp.float32),
            pltpu.VMEM((rows, BAND), jnp.float32),
            pltpu.VMEM((templ_count, BAND), jnp.float32),
        ]
        sources = (forwards, twists, table, strain, inv_asd, cutoff)
        forward, twist, table, mine, asd, keep = pl.pallas_call(
            prepare_kernel,
            out_shape=results,
            in_specs=[hbm] * 6,
            out_specs=[vmem] * 6,
            scratch_shapes=[pltpu.SMEM(cutoff.shape, jnp.int32), pltpu.SemaphoreType.DMA((6,))],
            compiler_params=params,
            cost_estimate=pl.CostEstimate(flops=0, bytes_accessed=4 * table.size, transcendentals=0),
        )(*[pltpu.with_memory_space_constraint(source, pltpu.HBM) for source in sources])
    else:
        device = lax.axis_index("freq")
        forward, twist, mine, asd = forwards[device], twists[device], strain, inv_asd[:, :BAND]
        keep = (jnp.arange(BAND, dtype=jnp.int32)[None, :] < cutoff[:, None]).astype(jnp.float32)
    by_templ = jnp.transpose(spectra[..., :BAND], (1, 2, 0, 3))
    single, forward, twist, table, asd, keep = lax.optimization_barrier((single, forward, twist, table, asd, keep))
    blocks = [mine, other, first, second, single] + [exchange(block, lambda i: i ^ 1) for block in (first, second, single)]
    if tiles_fit:
        parts = pl.pallas_call(
            spectrum_kernel,
            out_shape=[jax.ShapeDtypeStruct((2 * rows, BAND), jnp.float32)] * outer,
            in_specs=[vmem] * (len(blocks) + 3),
            out_specs=[vmem] * outer,
            compiler_params=params,
        )(*blocks, forward, twist, table)
    else:
        real, imag = partial_spectrum(blocks, forward, twist, table)
        parts = [jnp.concatenate([x[m * rows : (m + 1) * rows] for x in (real, imag)], 0) for m in range(outer)]
    parts, by_templ = lax.optimization_barrier((list(parts), by_templ))
    received = [exchange(parts[step], functools.partial(line, step=step)) for step in reversed(range(1, outer))]
    parts = parts[:1] + received
    if tiles_fit:
        outgoing = pl.pallas_call(
            section_kernel,
            out_shape=jax.ShapeDtypeStruct((device_count, rows, 128), jnp.bfloat16),
            in_specs=[vmem] * (outer + 5),
            out_specs=vmem,
            compiler_params=params,
        )(*parts, asd, keep, by_templ, twist, table)
    else:
        product = products(parts, asd, keep, by_templ)
        slots = section(product, table[:BAND, : 2 * side], twist[0, :rows], twist[1, :rows])
        slots = jnp.stack(slots).astype(jnp.bfloat16).reshape(2 * templ_count, rows, device_count, rows)
        outgoing = jnp.transpose(slots, (2, 1, 0, 3)).reshape(device_count, rows, -1)
    received = lax.all_to_all(outgoing, "freq", 0, 0, tiled=True).reshape(side, -1)
    if tiles_fit:
        series, peak = pl.pallas_call(
            last_kernel,
            out_shape=(
                jax.ShapeDtypeStruct((templ_count, 2, rows, side), jnp.float32),
                jax.ShapeDtypeStruct((rows, side), jnp.float32),
            ),
            in_specs=[vmem] * 2,
            out_specs=(vmem, vmem),
            compiler_params=params,
        )(received, table)
    else:
        both = jnp.stack(last_stage(received, table[:, : 2 * side], side * side))
        series = jnp.transpose(both.reshape(2, templ_count, rows, side), (1, 0, 2, 3))
        peak = jnp.max(series[:, 0] ** 2 + series[:, 1] ** 2, axis=0)
    return series, lax.pmax(peak, "tmpl")


def solution(mesh):
    in_specs = (P("freq", None), P("freq", None), P("freq", "tmpl", None, None), P("tmpl"))
    out_specs = (P("tmpl", None, "freq", None), P("freq", None))
    return jax.shard_map(
        functools.partial(local, mesh.shape["freq"]),
        mesh=mesh,
        in_specs=in_specs,
        out_specs=out_specs,
        check_vma=False,
    )
```

```python
import functools

import jax
import jax.numpy as jnp
import ml_dtypes
import numpy as np
from jax import lax
from jax.experimental import pallas as pl
from jax.experimental.pallas import tpu as pltpu
from jax.sharding import PartitionSpec as P

BAND = 256
CORES = 2
INNER = 4
LANES = 128
VMEM_LIMIT = 16 << 20


def angles(left, right, modulus):
    return 2.0 * np.pi / modulus * (left[:, None] * right[None, :] % modulus)


def split(table):
    high = table.astype(ml_dtypes.bfloat16)
    low = (table - high.astype(np.float64)).astype(ml_dtypes.bfloat16)
    return high, low


def rows_of(devices, rows):
    return (np.asarray(devices)[:, None] * rows + np.arange(rows)).reshape(-1)


def across(device):
    return device ^ (INNER - 1) * CORES ^ 1


def beside(device):
    chip = device // CORES
    return device ^ CORES * (1 + (chip + chip // 2 + device) % 2) ^ 1


def held_by(device):
    result = [device, device ^ 1]
    for here in (device, device ^ 1):
        result += [beside(here), beside(here) ^ 1, across(here)]
    return result


def line(device, step):
    return device ^ (INNER * CORES * step ^ 1 if step else 0)


def device_tables(count, rows, side):
    outer = count // (INNER * CORES)
    positions = np.arange(side)
    forward, twist = [], []
    for device in range(count):
        wanted = rows_of([line(device, step) for step in range(outer)], rows)
        held = rows_of(held_by(device), rows)
        angle = angles(wanted, held, side)
        forward.append(np.concatenate(split(np.concatenate([np.cos(angle), -np.sin(angle)]))))
        angle = angles(wanted, positions, side * side)
        twist.append(np.stack([np.cos(angle), np.sin(angle)]))
    return np.stack(forward), np.stack(twist).astype(np.float32)


def transform_table(side):
    angle = angles(np.arange(side), np.arange(side), side)
    cos_high, cos_low = split(np.cos(angle))
    sin_high, sin_low = split(np.sin(angle))
    columns = []
    for cos_part, sin_part, width in ((cos_high, sin_high, side), (cos_low, sin_low, BAND)):
        for start in range(0, width, LANES):
            columns += [x[:, start : start + LANES] for x in (cos_part, sin_part)]
    return np.concatenate(columns, 1)


def dot(left, right):
    return jnp.dot(left, right, preferred_element_type=jnp.float32)


def inner(left, right):
    return lax.dot_general(left, right, (((0,), (0,)), ((), ())), preferred_element_type=jnp.float32)


def halves(value):
    high = value.astype(jnp.bfloat16)
    return high, (value - high.astype(jnp.float32)).astype(jnp.bfloat16)


def turns(value):
    starts = range(0, value.shape[1], 2 * LANES)
    return tuple(
        jnp.concatenate([value[:, start + part : start + part + LANES] for start in starts], 1) for part in (0, LANES)
    )


def partial_spectrum(blocks, forward, twist, table):
    _, wanted, side = twist.shape
    high, low = halves(jnp.concatenate(blocks, 0))
    both = dot(forward, high)
    first = both[: 2 * wanted] + both[2 * wanted :] + dot(forward[: 2 * wanted], low)
    real, imag = first[:wanted], first[wanted:]
    turned = jnp.concatenate([real * twist[0] + imag * twist[1], imag * twist[0] - real * twist[1]], 0)
    high, low = halves(turned)
    both = dot(jnp.concatenate([high, low], 0), table[:, : 2 * BAND])
    second = both[: 2 * wanted] + both[2 * wanted :] + dot(high, table[:, 2 * side :])
    by_cos, by_sin = turns(second)
    return by_cos[:wanted] + by_sin[wanted:], by_cos[wanted:] - by_sin[:wanted]


def products(parts, asd, keep, spectra):
    templ_count, _, rows, _ = spectra.shape
    white = functools.reduce(jnp.add, parts)
    white_real, white_imag = white[:rows] * asd, white[rows:] * asd
    result = []
    for part in range(2):
        for templ in range(templ_count):
            spec_real = spectra[templ, 0].astype(jnp.float32)
            spec_imag = spectra[templ, 1].astype(jnp.float32)
            if part == 0:
                value = white_real * spec_real + white_imag * spec_imag
            else:
                value = white_imag * spec_real - white_real * spec_imag
            result.append(jnp.where(keep[templ : templ + 1] > 0, value, 0.0).astype(jnp.bfloat16))
    return jnp.concatenate(result, 0)


def section(product, table, twist_cos, twist_sin):
    rows = twist_cos.shape[0]
    group = product.shape[0] // 2
    by_cos, by_sin = turns(dot(product, table))
    real_part = by_cos[:group] - by_sin[group:]
    imag_part = by_sin[:group] + by_cos[group:]
    result = []
    for part in range(2):
        for start in range(0, group, rows):
            here = slice(start, start + rows)
            if part == 0:
                result.append(real_part[here] * twist_cos - imag_part[here] * twist_sin)
            else:
                result.append(real_part[here] * twist_sin + imag_part[here] * twist_cos)
    return result


def last_stage(received, table, total):
    turned = inner(received, table)
    by_cos, by_sin = turns(turned)
    group = turned.shape[0] // 2
    return (by_cos[:group] - by_sin[group:]) * (1.0 / total), (by_sin[:group] + by_cos[group:]) * (1.0 / total)


def spread(slots, rows):
    count = len(slots)
    group = lax.broadcasted_iota(jnp.int32, slots[0].shape, 1) // rows
    turned = [slots[0]] + [pltpu.roll(slots[s], s * rows, 1) for s in range(1, count)]
    result = [turned[-d % count] for d in range(count)]
    bit = 1
    while bit < count:
        moved = (group // bit) % 2 == 1
        result = [jnp.where(moved, result[d - bit], result[d]) for d in range(count)]
        bit *= 2
    return result


def prepare_kernel(
    forwards, twists, table, strain, inv_asd, cutoff, forward, twist, table_out, strain_out, asd, keep, limits, arrived
):
    device = lax.axis_index("freq")
    moves = (
        (cutoff, limits),
        (strain, strain_out),
        (forwards.at[device], forward),
        (twists.at[device], twist),
        (inv_asd.at[:, :BAND], asd),
        (table, table_out),
    )
    copies = [pltpu.make_async_copy(source, target, arrived.at[i]) for i, (source, target) in enumerate(moves)]
    for copy in copies:
        copy.start()
    copies[0].wait()
    band = lax.broadcasted_iota(jnp.int32, (1, BAND), 1)
    for templ in range(keep.shape[0]):
        keep[templ : templ + 1, :] = jnp.where(band < limits[templ], 1.0, 0.0)
    for copy in copies[1:]:
        copy.wait()


def spectrum_kernel(*refs):
    inputs = INNER * CORES + 3
    (*blocks, forward, twist, table), outs = refs[:inputs], refs[inputs:]
    real, imag = partial_spectrum([block[...] for block in blocks], forward[...], twist, table)
    rows = outs[0].shape[0] // 2
    for m, out in enumerate(outs):
        out[:rows] = real[m * rows : (m + 1) * rows]
        out[rows:] = imag[m * rows : (m + 1) * rows]


def section_kernel(*refs):
    *parts, asd, keep, spectra, twist, table, out = refs
    rows = asd.shape[0]
    product = products([part[...] for part in parts], asd[...], keep[...], spectra)
    for start in range(0, twist.shape[2], LANES):
        columns = slice(start, start + LANES)
        slots = section(
            product, table[:BAND, 2 * start : 2 * (start + LANES)], twist[0, :rows, columns], twist[1, :rows, columns]
        )
        for place, piece in enumerate(spread(slots, rows)):
            out[start // rows + place] = piece.astype(jnp.bfloat16)


def last_kernel(received, table, series, peak, held):
    templ_count, _, rows, side = series.shape
    device = lax.axis_index("freq")
    scale = 1.0 / (side * side)
    values = received[...]

    def slot(which):
        start = pl.multiple_of((which + device) % (2 * templ_count) * rows, rows)
        return held[pl.ds(start, rows), :LANES], held[pl.ds(start, rows), LANES:]

    for start in range(0, side, LANES):
        columns = slice(start, start + LANES)
        held[...] = inner(values, table[:, 2 * start : 2 * (start + LANES)])
        best = None
        for templ in range(templ_count):
            real_cos, real_sin = slot(templ)
            imag_cos, imag_sin = slot(templ_count + templ)
            real_part = (real_cos - imag_sin) * scale
            imag_part = (real_sin + imag_cos) * scale
            series[templ, 0, :, columns] = real_part
            series[templ, 1, :, columns] = imag_part
            power = real_part * real_part + imag_part * imag_part
            best = power if best is None else jnp.maximum(best, power)
        peak[:, columns] = best


def local(device_count, strain, inv_asd, spectra, cutoff):
    rows, side = strain.shape
    templ_count = spectra.shape[1]
    outer = device_count // (INNER * CORES)
    forwards, twists = (jnp.asarray(x) for x in device_tables(device_count, rows, side))
    table = jnp.asarray(transform_table(side))
    tiles_fit = rows % 16 == 0 and 2 * templ_count * rows == LANES and side % LANES == 0
    params = pltpu.CompilerParams(vmem_limit_bytes=VMEM_LIMIT)
    vmem = pl.BlockSpec(memory_space=pltpu.VMEM)
    hbm = pl.BlockSpec(memory_space=pltpu.HBM)

    def exchange(value, partner):
        return lax.ppermute(value, "freq", [(i, partner(i)) for i in range(device_count)])

    other = exchange(strain, lambda i: i ^ 1)
    first = exchange(strain, beside)
    second = exchange(other, beside)
    single = exchange(strain, across)
    if tiles_fit:
        results = [
            pltpu.VMEM(forwards.shape[1:], jnp.bfloat16),
            pltpu.VMEM(twists.shape[1:], jnp.float32),
            pltpu.VMEM(table.shape, jnp.bfloat16),
            pltpu.VMEM(strain.shape, jnp.float32),
            pltpu.VMEM((rows, BAND), jnp.float32),
            pltpu.VMEM((templ_count, BAND), jnp.float32),
        ]
        sources = (forwards, twists, table, strain, inv_asd, cutoff)
        forward, twist, table, mine, asd, keep = pl.pallas_call(
            prepare_kernel,
            out_shape=results,
            in_specs=[hbm] * 6,
            out_specs=[vmem] * 6,
            scratch_shapes=[pltpu.SMEM(cutoff.shape, jnp.int32), pltpu.SemaphoreType.DMA((6,))],
            compiler_params=params,
            cost_estimate=pl.CostEstimate(flops=0, bytes_accessed=4 * table.size, transcendentals=0),
        )(*[pltpu.with_memory_space_constraint(source, pltpu.HBM) for source in sources])
    else:
        device = lax.axis_index("freq")
        forward, twist, mine, asd = forwards[device], twists[device], strain, inv_asd[:, :BAND]
        keep = (jnp.arange(BAND, dtype=jnp.int32)[None, :] < cutoff[:, None]).astype(jnp.float32)
    by_templ = jnp.transpose(spectra[..., :BAND], (1, 2, 0, 3))
    single, forward, twist, table, asd, keep = lax.optimization_barrier((single, forward, twist, table, asd, keep))
    blocks = [mine, other, first, second, single] + [exchange(block, lambda i: i ^ 1) for block in (first, second, single)]
    if tiles_fit:
        parts = pl.pallas_call(
            spectrum_kernel,
            out_shape=[jax.ShapeDtypeStruct((2 * rows, BAND), jnp.float32)] * outer,
            in_specs=[vmem] * (len(blocks) + 3),
            out_specs=[vmem] * outer,
            compiler_params=params,
        )(*blocks, forward, twist, table)
    else:
        real, imag = partial_spectrum(blocks, forward, twist, table)
        parts = [jnp.concatenate([x[m * rows : (m + 1) * rows] for x in (real, imag)], 0) for m in range(outer)]
    parts, by_templ = lax.optimization_barrier((list(parts), by_templ))
    received = [exchange(parts[step], functools.partial(line, step=step)) for step in reversed(range(1, outer))]
    parts = parts[:1] + received
    if tiles_fit:
        outgoing = pl.pallas_call(
            section_kernel,
            out_shape=jax.ShapeDtypeStruct((device_count, rows, LANES), jnp.bfloat16),
            in_specs=[vmem] * (outer + 5),
            out_specs=vmem,
            compiler_params=params,
        )(*parts, asd, keep, by_templ, twist, table)
    else:
        product = products(parts, asd, keep, by_templ)
        slots = section(product, table[:BAND, : 2 * side], twist[0, :rows], twist[1, :rows])
        slots = jnp.stack(slots).astype(jnp.bfloat16).reshape(2 * templ_count, rows, device_count, rows)
        outgoing = jnp.transpose(slots, (2, 1, 0, 3)).reshape(device_count, rows, -1)
    received = lax.all_to_all(outgoing, "freq", 0, 0, tiled=True).reshape(side, -1)
    if tiles_fit:
        series, peak = pl.pallas_call(
            last_kernel,
            out_shape=(
                jax.ShapeDtypeStruct((templ_count, 2, rows, side), jnp.float32),
                jax.ShapeDtypeStruct((rows, side), jnp.float32),
            ),
            in_specs=[vmem] * 2,
            out_specs=(vmem, vmem),
            scratch_shapes=[pltpu.VMEM((LANES, 2 * LANES), jnp.float32)],
            compiler_params=params,
        )(received, table)
    else:
        both = jnp.stack(last_stage(received, table[:, : 2 * side], side * side))
        series = jnp.transpose(both.reshape(2, templ_count, rows, side), (1, 0, 2, 3))
        peak = jnp.max(series[:, 0] ** 2 + series[:, 1] ** 2, axis=0)
    return series, lax.pmax(peak, "tmpl")


def solution(mesh):
    in_specs = (P("freq", None), P("freq", None), P("freq", "tmpl", None, None), P("tmpl"))
    out_specs = (P("tmpl", None, "freq", None), P("freq", None))
    return jax.shard_map(
        functools.partial(local, mesh.shape["freq"]),
        mesh=mesh,
        in_specs=in_specs,
        out_specs=out_specs,
        check_vma=False,
    )
```

```python
import functools

import jax
import jax.numpy as jnp
import ml_dtypes
import numpy as np
from jax import lax
from jax.experimental import pallas as pl
from jax.experimental.pallas import tpu as pltpu
from jax.sharding import PartitionSpec as P

BAND = 256
CORES = 2
INNER = 4
LANES = 128
VMEM_LIMIT = 16 << 20


def angles(left, right, modulus):
    return 2.0 * np.pi / modulus * (left[:, None] * right[None, :] % modulus)


def split(table):
    high = table.astype(ml_dtypes.bfloat16)
    low = (table - high.astype(np.float64)).astype(ml_dtypes.bfloat16)
    return high, low


def rows_of(devices, rows):
    return (np.asarray(devices)[:, None] * rows + np.arange(rows)).reshape(-1)


def across(device):
    return device ^ (INNER - 1) * CORES ^ 1


def beside(device):
    chip = device // CORES
    return device ^ CORES * (1 + (chip + chip // 2 + device) % 2) ^ 1


def held_by(device):
    result = [device, device ^ 1]
    for here in (device, device ^ 1):
        result += [beside(here), beside(here) ^ 1, across(here)]
    return result


def line(device, step):
    return device ^ (INNER * CORES * step ^ 1 if step else 0)


def device_tables(count, rows, side):
    outer = count // (INNER * CORES)
    positions = np.arange(side)
    forward, twist = [], []
    for device in range(count):
        wanted = rows_of([line(device, step) for step in range(outer)], rows)
        held = rows_of(held_by(device), rows)
        angle = angles(wanted, held, side)
        forward.append(np.concatenate(split(np.concatenate([np.cos(angle), -np.sin(angle)]))))
        angle = angles(wanted, positions, side * side)
        twist.append(np.stack([np.cos(angle), np.sin(angle)]))
    return np.stack(forward), np.stack(twist).astype(np.float32)


def transform_table(side):
    angle = angles(np.arange(side), np.arange(side), side)
    cos_high, cos_low = split(np.cos(angle))
    sin_high, sin_low = split(np.sin(angle))
    columns = []
    for cos_part, sin_part, width in ((cos_high, sin_high, side), (cos_low, sin_low, BAND)):
        for start in range(0, width, LANES):
            columns += [x[:, start : start + LANES] for x in (cos_part, sin_part)]
    return np.concatenate(columns, 1)


def dot(left, right):
    return jnp.dot(left, right, preferred_element_type=jnp.float32)


def inner(left, right):
    return lax.dot_general(left, right, (((0,), (0,)), ((), ())), preferred_element_type=jnp.float32)


def halves(value):
    high = value.astype(jnp.bfloat16)
    return high, (value - high.astype(jnp.float32)).astype(jnp.bfloat16)


def turns(value):
    starts = range(0, value.shape[1], 2 * LANES)
    return tuple(
        jnp.concatenate([value[:, start + part : start + part + LANES] for start in starts], 1) for part in (0, LANES)
    )


def partial_spectrum(blocks, forward, twist, table):
    _, wanted, side = twist.shape
    high, low = halves(jnp.concatenate(blocks, 0))
    both = dot(forward, high)
    first = both[: 2 * wanted] + both[2 * wanted :] + dot(forward[: 2 * wanted], low)
    real, imag = first[:wanted], first[wanted:]
    turned = jnp.concatenate([real * twist[0] + imag * twist[1], imag * twist[0] - real * twist[1]], 0)
    high, low = halves(turned)
    both = dot(jnp.concatenate([high, low], 0), table[:, : 2 * BAND])
    second = both[: 2 * wanted] + both[2 * wanted :] + dot(high, table[:, 2 * side :])
    by_cos, by_sin = turns(second)
    return by_cos[:wanted] + by_sin[wanted:], by_cos[wanted:] - by_sin[:wanted]


def products(parts, asd, keep, spectra):
    templ_count, _, rows, _ = spectra.shape
    white = functools.reduce(jnp.add, [part.astype(jnp.float32) for part in parts])
    white_real, white_imag = white[:rows] * asd, white[rows:] * asd
    result = []
    for part in range(2):
        for templ in range(templ_count):
            spec_real = spectra[templ, 0].astype(jnp.float32)
            spec_imag = spectra[templ, 1].astype(jnp.float32)
            if part == 0:
                value = white_real * spec_real + white_imag * spec_imag
            else:
                value = white_imag * spec_real - white_real * spec_imag
            result.append(jnp.where(keep[templ : templ + 1] > 0, value, 0.0).astype(jnp.bfloat16))
    return jnp.concatenate(result, 0)


def section(product, table, twist_cos, twist_sin):
    rows = twist_cos.shape[0]
    group = product.shape[0] // 2
    by_cos, by_sin = turns(dot(product, table))
    real_part = by_cos[:group] - by_sin[group:]
    imag_part = by_sin[:group] + by_cos[group:]
    result = []
    for part in range(2):
        for start in range(0, group, rows):
            here = slice(start, start + rows)
            if part == 0:
                result.append(real_part[here] * twist_cos - imag_part[here] * twist_sin)
            else:
                result.append(real_part[here] * twist_sin + imag_part[here] * twist_cos)
    return result


def last_stage(received, table, total):
    turned = inner(received, table)
    by_cos, by_sin = turns(turned)
    group = turned.shape[0] // 2
    return (by_cos[:group] - by_sin[group:]) * (1.0 / total), (by_sin[:group] + by_cos[group:]) * (1.0 / total)


def spread(slots, rows):
    count = len(slots)
    group = lax.broadcasted_iota(jnp.int32, slots[0].shape, 1) // rows
    turned = [slots[0]] + [pltpu.roll(slots[s], s * rows, 1) for s in range(1, count)]
    result = [turned[-d % count] for d in range(count)]
    bit = 1
    while bit < count:
        moved = (group // bit) % 2 == 1
        result = [jnp.where(moved, result[d - bit], result[d]) for d in range(count)]
        bit *= 2
    return result


def prepare_kernel(
    forwards, twists, table, strain, inv_asd, cutoff, forward, twist, table_out, strain_out, asd, keep, limits, arrived
):
    device = lax.axis_index("freq")
    moves = (
        (cutoff, limits),
        (strain, strain_out),
        (forwards.at[device], forward),
        (twists.at[device], twist),
        (inv_asd.at[:, :BAND], asd),
        (table, table_out),
    )
    copies = [pltpu.make_async_copy(source, target, arrived.at[i]) for i, (source, target) in enumerate(moves)]
    for copy in copies:
        copy.start()
    copies[0].wait()
    band = lax.broadcasted_iota(jnp.int32, (1, BAND), 1)
    for templ in range(keep.shape[0]):
        keep[templ : templ + 1, :] = jnp.where(band < limits[templ], 1.0, 0.0)
    for copy in copies[1:]:
        copy.wait()


def spectrum_kernel(*refs):
    inputs = INNER * CORES + 3
    (*blocks, forward, twist, table), outs = refs[:inputs], refs[inputs:]
    real, imag = partial_spectrum([block[...] for block in blocks], forward[...], twist, table)
    rows = outs[0].shape[0] // 2
    for m, out in enumerate(outs):
        out[:rows] = real[m * rows : (m + 1) * rows].astype(out.dtype)
        out[rows:] = imag[m * rows : (m + 1) * rows].astype(out.dtype)


def section_kernel(*refs):
    *parts, asd, keep, spectra, twist, table, out = refs
    rows = asd.shape[0]
    product = products([part[...] for part in parts], asd[...], keep[...], spectra)
    for start in range(0, twist.shape[2], LANES):
        columns = slice(start, start + LANES)
        slots = section(
            product, table[:BAND, 2 * start : 2 * (start + LANES)], twist[0, :rows, columns], twist[1, :rows, columns]
        )
        for place, piece in enumerate(spread(slots, rows)):
            out[start // rows + place] = piece.astype(jnp.bfloat16)


def last_kernel(received, table, series, peak, held):
    templ_count, _, rows, side = series.shape
    device = lax.axis_index("freq")
    scale = 1.0 / (side * side)
    values = received[...]

    def slot(which):
        start = pl.multiple_of((which + device) % (2 * templ_count) * rows, rows)
        return held[pl.ds(start, rows), :LANES], held[pl.ds(start, rows), LANES:]

    for start in range(0, side, LANES):
        columns = slice(start, start + LANES)
        held[...] = inner(values, table[:, 2 * start : 2 * (start + LANES)])
        best = None
        for templ in range(templ_count):
            real_cos, real_sin = slot(templ)
            imag_cos, imag_sin = slot(templ_count + templ)
            real_part = (real_cos - imag_sin) * scale
            imag_part = (real_sin + imag_cos) * scale
            series[templ, 0, :, columns] = real_part
            series[templ, 1, :, columns] = imag_part
            power = real_part * real_part + imag_part * imag_part
            best = power if best is None else jnp.maximum(best, power)
        peak[:, columns] = best


def local(device_count, strain, inv_asd, spectra, cutoff):
    rows, side = strain.shape
    templ_count = spectra.shape[1]
    outer = device_count // (INNER * CORES)
    forwards, twists = (jnp.asarray(x) for x in device_tables(device_count, rows, side))
    table = jnp.asarray(transform_table(side))
    tiles_fit = rows % 16 == 0 and 2 * templ_count * rows == LANES and side % LANES == 0
    sent_as = [jnp.float32 if step < 1 else jnp.bfloat16 for step in range(outer)]
    params = pltpu.CompilerParams(vmem_limit_bytes=VMEM_LIMIT)
    vmem = pl.BlockSpec(memory_space=pltpu.VMEM)
    hbm = pl.BlockSpec(memory_space=pltpu.HBM)

    def exchange(value, partner):
        return lax.ppermute(value, "freq", [(i, partner(i)) for i in range(device_count)])

    other = exchange(strain, lambda i: i ^ 1)
    first = exchange(strain, beside)
    second = exchange(other, beside)
    single = exchange(strain, across)
    if tiles_fit:
        results = [
            pltpu.VMEM(forwards.shape[1:], jnp.bfloat16),
            pltpu.VMEM(twists.shape[1:], jnp.float32),
            pltpu.VMEM(table.shape, jnp.bfloat16),
            pltpu.VMEM(strain.shape, jnp.float32),
            pltpu.VMEM((rows, BAND), jnp.float32),
            pltpu.VMEM((templ_count, BAND), jnp.float32),
        ]
        sources = (forwards, twists, table, strain, inv_asd, cutoff)
        forward, twist, table, mine, asd, keep = pl.pallas_call(
            prepare_kernel,
            out_shape=results,
            in_specs=[hbm] * 6,
            out_specs=[vmem] * 6,
            scratch_shapes=[pltpu.SMEM(cutoff.shape, jnp.int32), pltpu.SemaphoreType.DMA((6,))],
            compiler_params=params,
            cost_estimate=pl.CostEstimate(flops=0, bytes_accessed=4 * table.size, transcendentals=0),
        )(*[pltpu.with_memory_space_constraint(source, pltpu.HBM) for source in sources])
    else:
        device = lax.axis_index("freq")
        forward, twist, mine, asd = forwards[device], twists[device], strain, inv_asd[:, :BAND]
        keep = (jnp.arange(BAND, dtype=jnp.int32)[None, :] < cutoff[:, None]).astype(jnp.float32)
    by_templ = jnp.transpose(spectra[..., :BAND], (1, 2, 0, 3))
    single, forward, twist, table, asd, keep = lax.optimization_barrier((single, forward, twist, table, asd, keep))
    blocks = [mine, other, first, second, single] + [exchange(block, lambda i: i ^ 1) for block in (first, second, single)]
    if tiles_fit:
        parts = pl.pallas_call(
            spectrum_kernel,
            out_shape=[jax.ShapeDtypeStruct((2 * rows, BAND), sent) for sent in sent_as],
            in_specs=[vmem] * (len(blocks) + 3),
            out_specs=[vmem] * outer,
            compiler_params=params,
        )(*blocks, forward, twist, table)
    else:
        real, imag = partial_spectrum(blocks, forward, twist, table)
        parts = [
            jnp.concatenate([x[m * rows : (m + 1) * rows] for x in (real, imag)], 0).astype(sent_as[m]) for m in range(outer)
        ]
    parts, by_templ = lax.optimization_barrier((list(parts), by_templ))
    received = [exchange(parts[step], functools.partial(line, step=step)) for step in reversed(range(1, outer))]
    parts = parts[:1] + received
    if tiles_fit:
        outgoing = pl.pallas_call(
            section_kernel,
            out_shape=jax.ShapeDtypeStruct((device_count, rows, LANES), jnp.bfloat16),
            in_specs=[vmem] * (outer + 5),
            out_specs=vmem,
            compiler_params=params,
        )(*parts, asd, keep, by_templ, twist, table)
    else:
        product = products(parts, asd, keep, by_templ)
        slots = section(product, table[:BAND, : 2 * side], twist[0, :rows], twist[1, :rows])
        slots = jnp.stack(slots).astype(jnp.bfloat16).reshape(2 * templ_count, rows, device_count, rows)
        outgoing = jnp.transpose(slots, (2, 1, 0, 3)).reshape(device_count, rows, -1)
    received = lax.all_to_all(outgoing, "freq", 0, 0, tiled=True).reshape(side, -1)
    if tiles_fit:
        series, peak = pl.pallas_call(
            last_kernel,
            out_shape=(
                jax.ShapeDtypeStruct((templ_count, 2, rows, side), jnp.float32),
                jax.ShapeDtypeStruct((rows, side), jnp.float32),
            ),
            in_specs=[vmem] * 2,
            out_specs=(vmem, vmem),
            scratch_shapes=[pltpu.VMEM((LANES, 2 * LANES), jnp.float32)],
            compiler_params=params,
        )(received, table)
    else:
        both = jnp.stack(last_stage(received, table[:, : 2 * side], side * side))
        series = jnp.transpose(both.reshape(2, templ_count, rows, side), (1, 0, 2, 3))
        peak = jnp.max(series[:, 0] ** 2 + series[:, 1] ** 2, axis=0)
    return series, lax.pmax(peak, "tmpl")


def solution(mesh):
    in_specs = (P("freq", None), P("freq", None), P("freq", "tmpl", None, None), P("tmpl"))
    out_specs = (P("tmpl", None, "freq", None), P("freq", None))
    return jax.shard_map(
        functools.partial(local, mesh.shape["freq"]),
        mesh=mesh,
        in_specs=in_specs,
        out_specs=out_specs,
        check_vma=False,
    )
```

```python
import functools

import jax
import jax.numpy as jnp
import ml_dtypes
import numpy as np
from jax import lax
from jax.experimental import pallas as pl
from jax.experimental.pallas import tpu as pltpu
from jax.sharding import PartitionSpec as P

BAND = 256
CORES = 2
INNER = 4
LANES = 128
VMEM_LIMIT = 16 << 20


def angles(left, right, modulus):
    return 2.0 * np.pi / modulus * (left[:, None] * right[None, :] % modulus)


def split(table):
    high = table.astype(ml_dtypes.bfloat16)
    low = (table - high.astype(np.float64)).astype(ml_dtypes.bfloat16)
    return high, low


def rows_of(devices, rows):
    return (np.asarray(devices)[:, None] * rows + np.arange(rows)).reshape(-1)


def across(device):
    return device ^ (INNER - 1) * CORES ^ 1


def beside(device):
    chip = device // CORES
    return device ^ CORES * (1 + (chip + chip // 2 + device) % 2) ^ 1


def held_by(device):
    result = [device, device ^ 1]
    for here in (device, device ^ 1):
        result += [beside(here), beside(here) ^ 1, across(here)]
    return result


def line(device, step):
    return device ^ (INNER * CORES * step ^ 1 if step else 0)


def device_tables(count, rows, side):
    outer = count // (INNER * CORES)
    positions = np.arange(side)
    forward, twist = [], []
    for device in range(count):
        wanted = rows_of([line(device, step) for step in range(outer)], rows)
        held = rows_of(held_by(device), rows)
        angle = angles(wanted, held, side)
        forward.append(np.concatenate(split(np.concatenate([np.cos(angle), -np.sin(angle)]))))
        angle = angles(wanted, positions, side * side)
        twist.append(np.stack([np.cos(angle), np.sin(angle)]))
    return np.stack(forward), np.stack(twist).astype(np.float32)


def transform_table(side):
    angle = angles(np.arange(side), np.arange(side), side)
    cos_high, cos_low = split(np.cos(angle))
    sin_high, sin_low = split(np.sin(angle))
    columns = []
    for cos_part, sin_part, width in ((cos_high, sin_high, side), (cos_low, sin_low, BAND)):
        for start in range(0, width, LANES):
            columns += [x[:, start : start + LANES] for x in (cos_part, sin_part)]
    return np.concatenate(columns, 1)


def dot(left, right):
    return jnp.dot(left, right, preferred_element_type=jnp.float32)


def inner(left, right):
    return lax.dot_general(left, right, (((0,), (0,)), ((), ())), preferred_element_type=jnp.float32)


def halves(value):
    high = value.astype(jnp.bfloat16)
    return high, (value - high.astype(jnp.float32)).astype(jnp.bfloat16)


def turns(value):
    starts = range(0, value.shape[1], 2 * LANES)
    return tuple(
        jnp.concatenate([value[:, start + part : start + part + LANES] for start in starts], 1) for part in (0, LANES)
    )


def partial_spectrum(blocks, forward, twist, table):
    _, wanted, side = twist.shape
    high, low = halves(jnp.concatenate(blocks, 0))
    both = dot(forward, high)
    first = both[: 2 * wanted] + both[2 * wanted :] + dot(forward[: 2 * wanted], low)
    real, imag = first[:wanted], first[wanted:]
    turned = jnp.concatenate([real * twist[0] + imag * twist[1], imag * twist[0] - real * twist[1]], 0)
    high, low = halves(turned)
    both = dot(jnp.concatenate([high, low], 0), table[:, : 2 * BAND])
    second = both[: 2 * wanted] + both[2 * wanted :] + dot(high, table[:, 2 * side :])
    by_cos, by_sin = turns(second)
    return by_cos[:wanted] + by_sin[wanted:], by_cos[wanted:] - by_sin[:wanted]


def products(parts, asd, keep, spectra):
    templ_count, _, rows, _ = spectra.shape
    white = functools.reduce(jnp.add, [part.astype(jnp.float32) for part in parts])
    white_real, white_imag = white[:rows] * asd, white[rows:] * asd
    result = []
    for part in range(2):
        for templ in range(templ_count):
            spec_real = spectra[templ, 0].astype(jnp.float32)
            spec_imag = spectra[templ, 1].astype(jnp.float32)
            if part == 0:
                value = white_real * spec_real + white_imag * spec_imag
            else:
                value = white_imag * spec_real - white_real * spec_imag
            result.append(jnp.where(keep[templ : templ + 1] > 0, value, 0.0).astype(jnp.bfloat16))
    return jnp.concatenate(result, 0)


def section(product, table, twist_cos, twist_sin):
    rows = twist_cos.shape[0]
    group = product.shape[0] // 2
    by_cos, by_sin = turns(dot(product, table))
    real_part = by_cos[:group] - by_sin[group:]
    imag_part = by_sin[:group] + by_cos[group:]
    result = []
    for part in range(2):
        for start in range(0, group, rows):
            here = slice(start, start + rows)
            if part == 0:
                result.append(real_part[here] * twist_cos - imag_part[here] * twist_sin)
            else:
                result.append(real_part[here] * twist_sin + imag_part[here] * twist_cos)
    return result


def last_stage(received, table, total):
    turned = inner(received, table)
    by_cos, by_sin = turns(turned)
    group = turned.shape[0] // 2
    return (by_cos[:group] - by_sin[group:]) * (1.0 / total), (by_sin[:group] + by_cos[group:]) * (1.0 / total)


def spread(slots, rows):
    count = len(slots)
    group = lax.broadcasted_iota(jnp.int32, slots[0].shape, 1) // rows
    turned = [slots[0]] + [pltpu.roll(slots[s], s * rows, 1) for s in range(1, count)]
    result = [turned[-d % count] for d in range(count)]
    bit = 1
    while bit < count:
        moved = (group // bit) % 2 == 1
        result = [jnp.where(moved, result[d - bit], result[d]) for d in range(count)]
        bit *= 2
    return result


def prepare_kernel(
    forwards, twists, strain, inv_asd, cutoff, forward, twist, strain_out, asd, keep, limits, arrived
):
    device = lax.axis_index("freq")
    moves = (
        (cutoff, limits),
        (strain, strain_out),
        (forwards.at[device], forward),
        (twists.at[device], twist),
        (inv_asd.at[:, :BAND], asd),
    )
    copies = [pltpu.make_async_copy(source, target, arrived.at[i]) for i, (source, target) in enumerate(moves)]
    for copy in copies:
        copy.start()
    copies[0].wait()
    band = lax.broadcasted_iota(jnp.int32, (1, BAND), 1)
    for templ in range(keep.shape[0]):
        keep[templ : templ + 1, :] = jnp.where(band < limits[templ], 1.0, 0.0)
    for copy in copies[1:]:
        copy.wait()


def spectrum_kernel(*refs):
    inputs = INNER * CORES + 3
    (*blocks, forward, twist, table), outs = refs[:inputs], refs[inputs:]
    real, imag = partial_spectrum([block[...] for block in blocks], forward[...], twist, table)
    rows = outs[0].shape[0] // 2
    for m, out in enumerate(outs):
        out[:rows] = real[m * rows : (m + 1) * rows].astype(out.dtype)
        out[rows:] = imag[m * rows : (m + 1) * rows].astype(out.dtype)


def section_kernel(*refs):
    *parts, asd, keep, spectra, twist, table, out = refs
    rows = asd.shape[0]
    product = products([part[...] for part in parts], asd[...], keep[...], spectra)
    for start in range(0, twist.shape[2], LANES):
        columns = slice(start, start + LANES)
        slots = section(
            product, table[:BAND, 2 * start : 2 * (start + LANES)], twist[0, :rows, columns], twist[1, :rows, columns]
        )
        for place, piece in enumerate(spread(slots, rows)):
            out[start // rows + place] = piece.astype(jnp.bfloat16)


def last_kernel(received, table, series, peak, held):
    templ_count, _, rows, side = series.shape
    device = lax.axis_index("freq")
    scale = 1.0 / (side * side)
    values = received[...]

    def slot(which):
        start = pl.multiple_of((which + device) % (2 * templ_count) * rows, rows)
        return held[pl.ds(start, rows), :LANES], held[pl.ds(start, rows), LANES:]

    for start in range(0, side, LANES):
        columns = slice(start, start + LANES)
        held[...] = inner(values, table[:, 2 * start : 2 * (start + LANES)])
        best = None
        for templ in range(templ_count):
            real_cos, real_sin = slot(templ)
            imag_cos, imag_sin = slot(templ_count + templ)
            real_part = (real_cos - imag_sin) * scale
            imag_part = (real_sin + imag_cos) * scale
            series[templ, 0, :, columns] = real_part
            series[templ, 1, :, columns] = imag_part
            power = real_part * real_part + imag_part * imag_part
            best = power if best is None else jnp.maximum(best, power)
        peak[:, columns] = best


def local(device_count, strain, inv_asd, spectra, cutoff):
    rows, side = strain.shape
    templ_count = spectra.shape[1]
    outer = device_count // (INNER * CORES)
    forwards, twists = (jnp.asarray(x) for x in device_tables(device_count, rows, side))
    table = jnp.asarray(transform_table(side))
    tiles_fit = rows % 16 == 0 and 2 * templ_count * rows == LANES and side % LANES == 0
    sent_as = [jnp.float32 if step < 1 else jnp.bfloat16 for step in range(outer)]
    params = pltpu.CompilerParams(vmem_limit_bytes=VMEM_LIMIT)
    vmem = pl.BlockSpec(memory_space=pltpu.VMEM)
    hbm = pl.BlockSpec(memory_space=pltpu.HBM)

    def exchange(value, partner):
        return lax.ppermute(value, "freq", [(i, partner(i)) for i in range(device_count)])

    other = exchange(strain, lambda i: i ^ 1)
    first = exchange(strain, beside)
    second = exchange(other, beside)
    single = exchange(strain, across)
    if tiles_fit:
        results = [
            pltpu.VMEM(forwards.shape[1:], jnp.bfloat16),
            pltpu.VMEM(twists.shape[1:], jnp.float32),
            pltpu.VMEM(strain.shape, jnp.float32),
            pltpu.VMEM((rows, BAND), jnp.float32),
            pltpu.VMEM((templ_count, BAND), jnp.float32),
        ]
        sources = (forwards, twists, strain, inv_asd, cutoff)
        forward, twist, mine, asd, keep = pl.pallas_call(
            prepare_kernel,
            out_shape=results,
            in_specs=[hbm] * 5,
            out_specs=[vmem] * 5,
            scratch_shapes=[pltpu.SMEM(cutoff.shape, jnp.int32), pltpu.SemaphoreType.DMA((5,))],
            compiler_params=params,
            cost_estimate=pl.CostEstimate(flops=0, bytes_accessed=4 * table.size, transcendentals=0),
        )(*[pltpu.with_memory_space_constraint(source, pltpu.HBM) for source in sources])
    else:
        device = lax.axis_index("freq")
        forward, twist, mine, asd = forwards[device], twists[device], strain, inv_asd[:, :BAND]
        keep = (jnp.arange(BAND, dtype=jnp.int32)[None, :] < cutoff[:, None]).astype(jnp.float32)
    by_templ = jnp.transpose(spectra[..., :BAND], (1, 2, 0, 3))
    single, forward, twist, table, asd, keep = lax.optimization_barrier((single, forward, twist, table, asd, keep))
    blocks = [mine, other, first, second, single] + [exchange(block, lambda i: i ^ 1) for block in (first, second, single)]
    if tiles_fit:
        parts = pl.pallas_call(
            spectrum_kernel,
            out_shape=[jax.ShapeDtypeStruct((2 * rows, BAND), sent) for sent in sent_as],
            in_specs=[vmem] * (len(blocks) + 3),
            out_specs=[vmem] * outer,
            compiler_params=params,
        )(*blocks, forward, twist, table)
    else:
        real, imag = partial_spectrum(blocks, forward, twist, table)
        parts = [
            jnp.concatenate([x[m * rows : (m + 1) * rows] for x in (real, imag)], 0).astype(sent_as[m]) for m in range(outer)
        ]
    parts, by_templ = lax.optimization_barrier((list(parts), by_templ))
    received = [exchange(parts[step], functools.partial(line, step=step)) for step in reversed(range(1, outer))]
    parts = parts[:1] + received
    if tiles_fit:
        outgoing = pl.pallas_call(
            section_kernel,
            out_shape=jax.ShapeDtypeStruct((device_count, rows, LANES), jnp.bfloat16),
            in_specs=[vmem] * (outer + 5),
            out_specs=vmem,
            compiler_params=params,
        )(*parts, asd, keep, by_templ, twist, table)
    else:
        product = products(parts, asd, keep, by_templ)
        slots = section(product, table[:BAND, : 2 * side], twist[0, :rows], twist[1, :rows])
        slots = jnp.stack(slots).astype(jnp.bfloat16).reshape(2 * templ_count, rows, device_count, rows)
        outgoing = jnp.transpose(slots, (2, 1, 0, 3)).reshape(device_count, rows, -1)
    received = lax.all_to_all(outgoing, "freq", 0, 0, tiled=True).reshape(side, -1)
    if tiles_fit:
        series, peak = pl.pallas_call(
            last_kernel,
            out_shape=(
                jax.ShapeDtypeStruct((templ_count, 2, rows, side), jnp.float32),
                jax.ShapeDtypeStruct((rows, side), jnp.float32),
            ),
            in_specs=[vmem] * 2,
            out_specs=(vmem, vmem),
            scratch_shapes=[pltpu.VMEM((LANES, 2 * LANES), jnp.float32)],
            compiler_params=params,
        )(received, table)
    else:
        both = jnp.stack(last_stage(received, table[:, : 2 * side], side * side))
        series = jnp.transpose(both.reshape(2, templ_count, rows, side), (1, 0, 2, 3))
        peak = jnp.max(series[:, 0] ** 2 + series[:, 1] ** 2, axis=0)
    return series, lax.pmax(peak, "tmpl")


def solution(mesh):
    in_specs = (P("freq", None), P("freq", None), P("freq", "tmpl", None, None), P("tmpl"))
    out_specs = (P("tmpl", None, "freq", None), P("freq", None))
    return jax.shard_map(
        functools.partial(local, mesh.shape["freq"]),
        mesh=mesh,
        in_specs=in_specs,
        out_specs=out_specs,
        check_vma=False,
    )
```

```python
import functools

import jax
import jax.numpy as jnp
import ml_dtypes
import numpy as np
from jax import lax
from jax.experimental import pallas as pl
from jax.experimental.pallas import tpu as pltpu
from jax.sharding import PartitionSpec as P

BAND = 256
CORES = 2
INNER = 4
LANES = 128
VMEM_LIMIT = 16 << 20


def angles(left, right, modulus):
    return 2.0 * np.pi / modulus * (left[:, None] * right[None, :] % modulus)


def split(table):
    high = table.astype(ml_dtypes.bfloat16)
    low = (table - high.astype(np.float64)).astype(ml_dtypes.bfloat16)
    return high, low


def rows_of(devices, rows):
    return (np.asarray(devices)[:, None] * rows + np.arange(rows)).reshape(-1)


def across(device):
    return device ^ (INNER - 1) * CORES ^ 1


def beside(device):
    chip = device // CORES
    return device ^ CORES * (1 + (chip + chip // 2 + device) % 2) ^ 1


def held_by(device):
    result = [device, device ^ 1]
    for here in (device, device ^ 1):
        result += [beside(here), beside(here) ^ 1, across(here)]
    return result


def line(device, step):
    return device ^ (INNER * CORES * step ^ 1 if step else 0)


def device_tables(count, rows, side):
    outer = count // (INNER * CORES)
    positions = np.arange(side)
    forward, twist = [], []
    for device in range(count):
        wanted = rows_of([line(device, step) for step in range(outer)], rows)
        held = rows_of(held_by(device), rows)
        angle = angles(wanted, held, side)
        forward.append(np.concatenate(split(np.concatenate([np.cos(angle), -np.sin(angle)]))))
        angle = angles(wanted, positions, side * side)
        twist.append(np.stack([np.cos(angle), np.sin(angle)]))
    return np.stack(forward), np.stack(twist).astype(np.float32)


def transform_table(side):
    angle = angles(np.arange(side), np.arange(side), side)
    cos_high, cos_low = split(np.cos(angle))
    sin_high, sin_low = split(np.sin(angle))
    columns = []
    for cos_part, sin_part, width in ((cos_high, sin_high, side), (cos_low, sin_low, BAND)):
        for start in range(0, width, LANES):
            columns += [x[:, start : start + LANES] for x in (cos_part, sin_part)]
    return np.concatenate(columns, 1)


def dot(left, right):
    return jnp.dot(left, right, preferred_element_type=jnp.float32)


def inner(left, right):
    return lax.dot_general(left, right, (((0,), (0,)), ((), ())), preferred_element_type=jnp.float32)


def halves(value):
    high = value.astype(jnp.bfloat16)
    return high, (value - high.astype(jnp.float32)).astype(jnp.bfloat16)


def turns(value):
    starts = range(0, value.shape[1], 2 * LANES)
    return tuple(
        jnp.concatenate([value[:, start + part : start + part + LANES] for start in starts], 1) for part in (0, LANES)
    )


def partial_spectrum(blocks, forward, twist, table):
    _, wanted, side = twist.shape
    high, low = halves(jnp.concatenate(blocks, 0))
    both = dot(forward, high)
    first = both[: 2 * wanted] + both[2 * wanted :] + dot(forward[: 2 * wanted], low)
    real, imag = first[:wanted], first[wanted:]
    turned = jnp.concatenate([real * twist[0] + imag * twist[1], imag * twist[0] - real * twist[1]], 0)
    high, low = halves(turned)
    both = dot(jnp.concatenate([high, low], 0), table[:, : 2 * BAND])
    second = both[: 2 * wanted] + both[2 * wanted :] + dot(high, table[:, 2 * side :])
    by_cos, by_sin = turns(second)
    return by_cos[:wanted] + by_sin[wanted:], by_cos[wanted:] - by_sin[:wanted]


def products(parts, asd, keep, spectra):
    templ_count, _, rows, _ = spectra.shape
    white = functools.reduce(jnp.add, [part.astype(jnp.float32) for part in parts])
    white_real, white_imag = white[:rows] * asd, white[rows:] * asd
    result = []
    for part in range(2):
        for templ in range(templ_count):
            spec_real = spectra[templ, 0].astype(jnp.float32)
            spec_imag = spectra[templ, 1].astype(jnp.float32)
            if part == 0:
                value = white_real * spec_real + white_imag * spec_imag
            else:
                value = white_imag * spec_real - white_real * spec_imag
            result.append(jnp.where(keep[templ : templ + 1] > 0, value, 0.0).astype(jnp.bfloat16))
    return jnp.concatenate(result, 0)


def section(product, table, twist_cos, twist_sin):
    rows = twist_cos.shape[0]
    group = product.shape[0] // 2
    by_cos, by_sin = turns(dot(product, table))
    real_part = by_cos[:group] - by_sin[group:]
    imag_part = by_sin[:group] + by_cos[group:]
    result = []
    for part in range(2):
        for start in range(0, group, rows):
            here = slice(start, start + rows)
            if part == 0:
                result.append(real_part[here] * twist_cos - imag_part[here] * twist_sin)
            else:
                result.append(real_part[here] * twist_sin + imag_part[here] * twist_cos)
    return result


def last_stage(received, table, total):
    turned = inner(received, table)
    by_cos, by_sin = turns(turned)
    group = turned.shape[0] // 2
    return (by_cos[:group] - by_sin[group:]) * (1.0 / total), (by_sin[:group] + by_cos[group:]) * (1.0 / total)


def spread(slots, rows):
    count = len(slots)
    group = lax.broadcasted_iota(jnp.int32, slots[0].shape, 1) // rows
    turned = [slots[0]] + [pltpu.roll(slots[s], s * rows, 1) for s in range(1, count)]
    result = [turned[-d % count] for d in range(count)]
    bit = 1
    while bit < count:
        moved = (group // bit) % 2 == 1
        result = [jnp.where(moved, result[d - bit], result[d]) for d in range(count)]
        bit *= 2
    return result


def prepare_kernel(
    forwards, twists, table, strain, inv_asd, cutoff, forward, twist, table_out, strain_out, asd, keep, limits, arrived
):
    device = lax.axis_index("freq")
    moves = (
        (cutoff, limits),
        (strain, strain_out),
        (forwards.at[device], forward),
        (twists.at[device], twist),
        (inv_asd.at[:, :BAND], asd),
        (table, table_out),
    )
    copies = [pltpu.make_async_copy(source, target, arrived.at[i]) for i, (source, target) in enumerate(moves)]
    for copy in copies:
        copy.start()
    copies[0].wait()
    band = lax.broadcasted_iota(jnp.int32, (1, BAND), 1)
    for templ in range(keep.shape[0]):
        keep[templ : templ + 1, :] = jnp.where(band < limits[templ], 1.0, 0.0)
    for copy in copies[1:]:
        copy.wait()


def spectrum_kernel(*refs):
    inputs = INNER * CORES + 3
    (*blocks, forward, twist, table), outs = refs[:inputs], refs[inputs:]
    real, imag = partial_spectrum([block[...] for block in blocks], forward[...], twist, table)
    rows = outs[0].shape[0] // 2
    for m, out in enumerate(outs):
        out[:rows] = real[m * rows : (m + 1) * rows].astype(out.dtype)
        out[rows:] = imag[m * rows : (m + 1) * rows].astype(out.dtype)


def section_kernel(*refs):
    *parts, asd, keep, spectra, twist, table, out = refs
    rows = asd.shape[0]
    product = products([part[...] for part in parts], asd[...], keep[...], spectra)
    for start in range(0, twist.shape[2], LANES):
        columns = slice(start, start + LANES)
        slots = section(
            product, table[:BAND, 2 * start : 2 * (start + LANES)], twist[0, :rows, columns], twist[1, :rows, columns]
        )
        for place, piece in enumerate(spread(slots, rows)):
            out[start // rows + place] = piece.astype(jnp.bfloat16)


def last_kernel(received, table, series, peak, held):
    templ_count, _, rows, side = series.shape
    device = lax.axis_index("freq")
    scale = 1.0 / (side * side)
    values = received[...]

    def slot(which):
        start = pl.multiple_of((which + device) % (2 * templ_count) * rows, rows)
        return held[pl.ds(start, rows), :LANES], held[pl.ds(start, rows), LANES:]

    for start in range(0, side, LANES):
        columns = slice(start, start + LANES)
        held[...] = inner(values, table[:, 2 * start : 2 * (start + LANES)])
        best = None
        for templ in range(templ_count):
            real_cos, real_sin = slot(templ)
            imag_cos, imag_sin = slot(templ_count + templ)
            real_part = (real_cos - imag_sin) * scale
            imag_part = (real_sin + imag_cos) * scale
            series[templ, 0, :, columns] = real_part
            series[templ, 1, :, columns] = imag_part
            power = real_part * real_part + imag_part * imag_part
            best = power if best is None else jnp.maximum(best, power)
        peak[:, columns] = best


def local(device_count, strain, inv_asd, spectra, cutoff):
    rows, side = strain.shape
    templ_count = spectra.shape[1]
    outer = device_count // (INNER * CORES)
    forwards, twists = (jnp.asarray(x) for x in device_tables(device_count, rows, side))
    table = jnp.asarray(transform_table(side))
    tiles_fit = rows % 16 == 0 and 2 * templ_count * rows == LANES and side % LANES == 0
    sent_as = [jnp.float32 if step < 1 else jnp.bfloat16 for step in range(outer)]
    params = pltpu.CompilerParams(vmem_limit_bytes=VMEM_LIMIT)
    vmem = pl.BlockSpec(memory_space=pltpu.VMEM)
    hbm = pl.BlockSpec(memory_space=pltpu.HBM)

    def exchange(value, partner):
        return lax.ppermute(value, "freq", [(i, partner(i)) for i in range(device_count)])

    other = exchange(strain, lambda i: i ^ 1)
    first = exchange(strain, beside)
    second = exchange(other, beside)
    single = exchange(strain, across)
    if tiles_fit:
        results = [
            pltpu.VMEM(forwards.shape[1:], jnp.bfloat16),
            pltpu.VMEM(twists.shape[1:], jnp.float32),
            pltpu.VMEM(table.shape, jnp.bfloat16),
            pltpu.VMEM(strain.shape, jnp.float32),
            pltpu.VMEM((rows, BAND), jnp.float32),
            pltpu.VMEM((templ_count, BAND), jnp.float32),
        ]
        sources = (forwards, twists, table, strain, inv_asd, cutoff)
        forward, twist, table, mine, asd, keep = pl.pallas_call(
            prepare_kernel,
            out_shape=results,
            in_specs=[hbm] * 6,
            out_specs=[vmem] * 6,
            scratch_shapes=[pltpu.SMEM(cutoff.shape, jnp.int32), pltpu.SemaphoreType.DMA((6,))],
            compiler_params=params,
            cost_estimate=pl.CostEstimate(flops=0, bytes_accessed=4 * table.size, transcendentals=0),
        )(*[pltpu.with_memory_space_constraint(source, pltpu.HBM) for source in sources])
    else:
        device = lax.axis_index("freq")
        forward, twist, mine, asd = forwards[device], twists[device], strain, inv_asd[:, :BAND]
        keep = (jnp.arange(BAND, dtype=jnp.int32)[None, :] < cutoff[:, None]).astype(jnp.float32)
    by_templ = jnp.transpose(spectra[..., :BAND], (1, 2, 0, 3))
    single, forward, twist, table, asd, keep = lax.optimization_barrier((single, forward, twist, table, asd, keep))
    blocks = [mine, other, first, second, single] + [exchange(block, lambda i: i ^ 1) for block in (first, second, single)]
    if tiles_fit:
        parts = pl.pallas_call(
            spectrum_kernel,
            out_shape=[jax.ShapeDtypeStruct((2 * rows, BAND), sent) for sent in sent_as],
            in_specs=[vmem] * (len(blocks) + 3),
            out_specs=[vmem] * outer,
            compiler_params=params,
        )(*blocks, forward, twist, table)
    else:
        real, imag = partial_spectrum(blocks, forward, twist, table)
        parts = [
            jnp.concatenate([x[m * rows : (m + 1) * rows] for x in (real, imag)], 0).astype(sent_as[m]) for m in range(outer)
        ]
    parts = list(parts)
    received = [exchange(parts[step], functools.partial(line, step=step)) for step in reversed(range(1, outer))]
    parts = parts[:1] + received
    if tiles_fit:
        outgoing = pl.pallas_call(
            section_kernel,
            out_shape=jax.ShapeDtypeStruct((device_count, rows, LANES), jnp.bfloat16),
            in_specs=[vmem] * (outer + 5),
            out_specs=vmem,
            compiler_params=params,
        )(*parts, asd, keep, by_templ, twist, table)
    else:
        product = products(parts, asd, keep, by_templ)
        slots = section(product, table[:BAND, : 2 * side], twist[0, :rows], twist[1, :rows])
        slots = jnp.stack(slots).astype(jnp.bfloat16).reshape(2 * templ_count, rows, device_count, rows)
        outgoing = jnp.transpose(slots, (2, 1, 0, 3)).reshape(device_count, rows, -1)
    received = lax.all_to_all(outgoing, "freq", 0, 0, tiled=True).reshape(side, -1)
    if tiles_fit:
        series, peak = pl.pallas_call(
            last_kernel,
            out_shape=(
                jax.ShapeDtypeStruct((templ_count, 2, rows, side), jnp.float32),
                jax.ShapeDtypeStruct((rows, side), jnp.float32),
            ),
            in_specs=[vmem] * 2,
            out_specs=(vmem, vmem),
            scratch_shapes=[pltpu.VMEM((LANES, 2 * LANES), jnp.float32)],
            compiler_params=params,
        )(received, table)
    else:
        both = jnp.stack(last_stage(received, table[:, : 2 * side], side * side))
        series = jnp.transpose(both.reshape(2, templ_count, rows, side), (1, 0, 2, 3))
        peak = jnp.max(series[:, 0] ** 2 + series[:, 1] ** 2, axis=0)
    return series, lax.pmax(peak, "tmpl")


def solution(mesh):
    in_specs = (P("freq", None), P("freq", None), P("freq", "tmpl", None, None), P("tmpl"))
    out_specs = (P("tmpl", None, "freq", None), P("freq", None))
    return jax.shard_map(
        functools.partial(local, mesh.shape["freq"]),
        mesh=mesh,
        in_specs=in_specs,
        out_specs=out_specs,
        check_vma=False,
    )
```
